256 devices in a mesh: row: 4 (over y), theta: 16 (over z, x_lo), axial: 4 (over x_hi, core).
Axes of the slice: x: 4 (x_hi: 2, x_lo: 2; x = x_hi * 2 + x_lo), y: 4, z: 8, core: 2. Of those that a mesh axis runs over, the one named last changes fastest.
Arguments:
- adjoint_state: float32 [4, 2, 5, 32, 512, 128], P('row', None, None, 'axial', 'theta'), may hold values from -6 to 6
- source: float32 [4, 2, 5, 32, 512, 128], P('row', None, None, 'axial', 'theta'), may hold values from -6 to 6
- time_step: float32 [4, 32, 512, 128], P('row', 'axial', 'theta'), may hold values from 0.05 to 0.25
- flux_jacobian: float32 [4, 3, 5, 5, 32, 128], P('row', None, None, None, 'axial'), may hold values from -2.5 to 2.5
- blade_count: int32 [4], P('row'), may hold values from 16 to 79
- mode_order: int32 [4, 512], P('row'), may hold values from 0 to 511, each once within a row
- giles_matrix: float32 [4, 2, 2, 2, 5, 5], P('row'), may hold values from -4.2 to 4.2
- coupling_matrix: float32 [4, 2, 2, 5, 5], P('row'), may hold values from -9 to 9
Outputs:
- new_state: float32 [4, 2, 5, 32, 512, 128], P('row', None, None, 'axial', 'theta')
The draws below stay inside these ranges and needn't reach their ends.
Inputs may be any that keep to these rules, and one draw needn't show every extreme that they name: Each row of mode_order lists every number 0 to 511 once.
All inputs are finite; a program needn't handle non-finite values.
Results may differ from the reference program's by a relative error of at most 0.0001.
Values sent between devices are 32-bit elements; how exact they have to be, the bound alone decides.
A program may use at most 128 MiB of HBM per device.

```python
import math
import jax
import jax.numpy as jnp
from jax import lax

ROWS = 4
NR = 128
MODES = 16
SECTIONS = 4
NTH = 512
NAX = 32


def with_ends(array, rng, smallest, high):
    shape = array.shape
    spot = [jax.random.randint(jax.random.fold_in(rng, axis), (), 0, shape[axis]) for axis in range(len(shape))]
    array = array.at[tuple(spot)].set(smallest)
    longest = shape.index(max(shape))
    spot[longest] = (spot[longest] + 1) % shape[longest]
    return array.at[tuple(spot)].set(high)


def level_of(rng, shape, shards, low, top_value):
    def one(axis_at, shards_of):
        steps = jax.random.uniform(jax.random.fold_in(jax.random.fold_in(rng, 6), axis_at), (shards_of,), jnp.float32, low / len(shards), top_value / len(shards))
        return jnp.repeat(jnp.exp(steps), shape[axis_at] // shards_of).reshape((-1,) + (1,) * (len(shape) - axis_at - 1))

    loudness = one(*shards[0])
    for cut in shards[1:]:
        loudness = loudness * one(*cut)
    return loudness


def gaussian(rng, dims, width, bound, pieces=(), kind=jnp.bfloat16):
    values = width * jax.random.normal(rng, dims, jnp.float32)
    if pieces:
        values = values * level_of(rng, dims, pieces, -0.22, 0.18)
    return jnp.clip(values, -bound, bound).astype(kind)


def setup_inputs(seed: int = 0) -> dict:
    arg_keys = jax.random.split(jax.random.key(seed), 9)
    adjoint_state = gaussian(arg_keys[0], (ROWS, 2, 5, NAX, NTH, NR), 1.0, 6.0, ((0, 4), (3, 4), (4, 16)), jnp.float32)
    source = gaussian(arg_keys[1], (ROWS, 2, 5, NAX, NTH, NR), 1.0, 6.0, ((0, 4), (3, 4), (4, 16)), jnp.float32)
    time_step = jnp.clip(jnp.exp(math.log(0.25) - 1.609438 * jax.random.uniform(arg_keys[2], (ROWS, NAX, NTH, NR), jnp.float32) ** level_of(arg_keys[2], (ROWS, NAX, NTH, NR), ((0, 4), (1, 4), (2, 16)), -0.2, 0.2)), 0.05, 0.25)
    flux_jacobian = gaussian(arg_keys[3], (ROWS, 3, 5, 5, NAX, NR), 5 ** -0.5, 2.5, ((0, 4), (4, 4)), jnp.float32)
    blade_count = with_ends(jax.random.randint(arg_keys[4], (ROWS,), 16, 80), jax.random.fold_in(arg_keys[4], 1), 16, 79).astype(jnp.int32)
    mode_order = jax.vmap(lambda own: jax.random.permutation(own, NTH))(jax.random.split(arg_keys[5], ROWS)).reshape((ROWS, NTH)).astype(jnp.int32)
    giles_matrix = gaussian(arg_keys[6], (ROWS, 2, 2, 2, 5, 5), 0.7, 4.2, ((0, 4),), jnp.float32)
    coupling_matrix = gaussian(arg_keys[7], (ROWS, 2, 2, 5, 5), 1.5, 9.0, ((0, 4),), jnp.float32)
    return dict(adjoint_state=adjoint_state, source=source, time_step=time_step, flux_jacobian=flux_jacobian, blade_count=blade_count, mode_order=mode_order, giles_matrix=giles_matrix, coupling_matrix=coupling_matrix)


DISSIPATION = 0.05
OMEGA_UNIT = 0.02
HIGHEST = lax.Precision.HIGHEST


def shift_radius(field, upward):
    zero_layer = jnp.zeros(field.shape[:-1] + (1,), jnp.float32)
    if upward:
        return jnp.concatenate([field[..., 1:], zero_layer], -1)
    return jnp.concatenate([zero_layer, field[..., :-1]], -1)


def mode_tables(order_row, columns, circle, retained):
    mode_numbers = order_row[:retained] - circle // 2
    angles = jnp.mod(mode_numbers[:, None] * columns[None, :], circle).astype(jnp.float32) * (2.0 * math.pi / circle)
    return mode_numbers, jnp.cos(angles), jnp.sin(angles)


def forward_transform(cosine, sine_table, field, circle):
    real_part = jnp.einsum("mj,kjr->kmr", cosine, field[0], precision=HIGHEST) + jnp.einsum("mj,kjr->kmr", sine_table, field[1], precision=HIGHEST)
    imag_part = jnp.einsum("mj,kjr->kmr", cosine, field[1], precision=HIGHEST) - jnp.einsum("mj,kjr->kmr", sine_table, field[0], precision=HIGHEST)
    return jnp.stack([real_part, imag_part]) / circle


def inverse_transform(cosine, sine_table, coeffs):
    real_part = jnp.einsum("mj,kmr->kjr", cosine, coeffs[0], precision=HIGHEST) - jnp.einsum("mj,kmr->kjr", sine_table, coeffs[1], precision=HIGHEST)
    imag_part = jnp.einsum("mj,kmr->kjr", sine_table, coeffs[0], precision=HIGHEST) + jnp.einsum("mj,kmr->kjr", cosine, coeffs[1], precision=HIGHEST)
    return jnp.stack([real_part, imag_part])


def apply_matrix(matrix, vector):
    real_part = jnp.einsum("cv,vmr->cmr", matrix[0], vector[0], precision=HIGHEST) - jnp.einsum("cv,vmr->cmr", matrix[1], vector[1], precision=HIGHEST)
    imag_part = jnp.einsum("cv,vmr->cmr", matrix[0], vector[1], precision=HIGHEST) + jnp.einsum("cv,vmr->cmr", matrix[1], vector[0], precision=HIGHEST)
    return jnp.stack([real_part, imag_part])


def boundary_modes(giles_pair, coupling, coeffs, neighbour, mode_scale):
    result = apply_matrix(giles_pair[0], coeffs)
    result = result + mode_scale[None, None, :, None] * apply_matrix(giles_pair[1], coeffs)
    return result + apply_matrix(coupling, neighbour)


def interior(field, jacobian, frequency):
    zero_plane = jnp.zeros_like(field[:, :, :1])
    axial_next = jnp.concatenate([field[:, :, 1:], zero_plane], 2)
    axial_prev = jnp.concatenate([zero_plane, field[:, :, :-1]], 2)
    theta_next = jnp.roll(field, -1, 3)
    theta_prev = jnp.roll(field, 1, 3)
    radial_next = shift_radius(field, True)
    radial_prev = shift_radius(field, False)
    deltas = ((axial_next - axial_prev) * 0.5, (theta_next - theta_prev) * 0.5, (radial_next - radial_prev) * 0.5)
    flux_sum = jnp.zeros_like(field)
    for direction in range(3):
        for variable in range(5):
            flux_sum = flux_sum + jacobian[direction, variable][None, :, :, None, :] * deltas[direction][:, variable][:, None]
    rotated = jnp.stack([field[1], -field[0]])
    laplacian = axial_next + axial_prev + theta_next + theta_prev + radial_next + radial_prev - 6.0 * field
    return flux_sum + frequency * rotated + DISSIPATION * laplacian


def reference(adjoint_state, source, time_step, flux_jacobian, blade_count, mode_order, giles_matrix, coupling_matrix):
    columns = jnp.arange(NTH, dtype=jnp.int32)
    row_tables = [mode_tables(mode_order[row_index], columns, NTH, MODES) for row_index in range(ROWS)]
    current = [adjoint_state[row_index] for row_index in range(ROWS)]
    for section_index in range(SECTIONS):
        weight = 1.0 / (SECTIONS - section_index)
        inlet_modes = [forward_transform(row_tables[row_index][1], row_tables[row_index][2], current[row_index][:, :, 0], NTH) for row_index in range(ROWS)]
        outlet_modes = [forward_transform(row_tables[row_index][1], row_tables[row_index][2], current[row_index][:, :, -1], NTH) for row_index in range(ROWS)]
        updated = []
        for row_index in range(ROWS):
            mode_numbers, cosine, sine_table = row_tables[row_index]
            mode_scale = 2.0 * mode_numbers.astype(jnp.float32) / NTH
            zero_modes = jnp.zeros_like(inlet_modes[row_index])
            upstream = outlet_modes[row_index - 1] if row_index > 0 else zero_modes
            downstream = inlet_modes[row_index + 1] if row_index < ROWS - 1 else zero_modes
            inlet_fix = inverse_transform(cosine, sine_table, boundary_modes(giles_matrix[row_index, 0], coupling_matrix[row_index, 0], inlet_modes[row_index], upstream, mode_scale))
            outlet_fix = inverse_transform(cosine, sine_table, boundary_modes(giles_matrix[row_index, 1], coupling_matrix[row_index, 1], outlet_modes[row_index], downstream, mode_scale))
            frequency = blade_count[row_index].astype(jnp.float32) * OMEGA_UNIT
            residual = source[row_index] + interior(current[row_index], flux_jacobian[row_index], frequency)
            residual = residual.at[:, :, 0].add(-inlet_fix)
            residual = residual.at[:, :, -1].add(-outlet_fix)
            updated.append(adjoint_state[row_index] + weight * time_step[row_index] * residual)
        current = updated
    return jnp.stack(current)
```

```python
import functools
import math

import jax
import jax.numpy as jnp
from jax import lax
from jax.experimental import pallas as pl
from jax.experimental.pallas import tpu as pltpu
from jax.sharding import PartitionSpec as P

MESH = pl.DeviceIdType.MESH
F32 = jnp.float32
BF16 = jnp.bfloat16
MODES = 16
SECTIONS = 4
DISSIPATION = 0.05
OMEGA_UNIT = 0.02
LAYERS = 8
SECTOR = 32
RADII = 128
VARS = 5
PAD = 16
FIRST, LAST = PAD, PAD + SECTOR - 1
OWN = pl.ds(PAD, SECTOR)
BAND = 8
WIDE = 384
MODE_ROW = 100


def sin_cos(turns):
    h = (turns - jnp.floor(turns + 0.5)) * math.pi
    z = h * h
    s = 1.0 / 6227020800
    for d in (-39916800, 362880, -5040, 120, -6, 1):
        s = s * z + 1.0 / d
    s = s * h
    c = 1.0 / 479001600
    for d in (-3628800, 40320, -720, 24, -2, 1):
        c = c * z + 1.0 / d
    return 2.0 * s * c, 1.0 - 2.0 * s * s


def high(x):
    return x.astype(BF16).astype(F32)


def lanes(rows):
    return lax.broadcasted_iota(jnp.int32, (rows, 128), 1)


def subs(rows):
    return lax.broadcasted_iota(jnp.int32, (rows, 128), 0)


def wait_for(ref, sem):
    pltpu.make_async_copy(ref, ref, sem).wait()


def kernel(
    shape,
    state_in,
    source_in,
    step_in,
    jac_in,
    blade,
    order,
    giles,
    coupling,
    out,
    v,
    src,
    dt,
    jin,
    jb,
    t_out,
    t_in,
    wf,
    w2,
    e_tab,
    pack,
    parts,
    sent,
    got,
    dt_all,
    c_out,
    c_in,
    load_sem,
    th_send,
    th_recv,
    ax_send,
    ax_recv,
    dt_send,
    dt_recv,
    pk_sem,
    p_send,
    p_recv,
    c_send,
    c_recv,
    out_sem,
):
    nrow, nth, nax, circle = shape
    y, t, a = lax.axis_index("row"), lax.axis_index("theta"), lax.axis_index("axial")
    inlet, outlet = a == 0, a == nax - 1
    bnd = jnp.logical_or(inlet, outlet)
    inner = jnp.logical_not(bnd)
    side = jnp.where(inlet, 0, 1)
    paired = jnp.logical_or(
        jnp.logical_and(inlet, y > 0), jnp.logical_and(outlet, y < nrow - 1)
    )
    alone = jnp.logical_not(paired)
    py = jnp.where(paired, jnp.where(inlet, y - 1, y + 1), y)
    pa = jnp.where(paired, jnp.where(inlet, nax - 1, 0), a)
    edge = jnp.where(inlet, 1, LAYERS)

    def on_my_side(band):
        return jnp.logical_or(alone, lax.rem(band // 2, 2) == side)

    owner = jnp.logical_and(bnd, on_my_side(t))
    t_next, t_prev = lax.rem(t + 1, nth), lax.rem(t + nth - 1, nth)

    load_state = pltpu.make_async_copy(
        state_in.at[0], v.at[0, :, :, pl.ds(1, LAYERS), OWN], load_sem.at[0]
    )
    load_step = pltpu.make_async_copy(step_in.at[0], dt.at[:, OWN], load_sem.at[1])
    load_jac = pltpu.make_async_copy(jac_in.at[0], jin, load_sem.at[2])
    load_source = pltpu.make_async_copy(source_in.at[0], src, load_sem.at[3])
    load_state.start()
    load_step.start()
    load_jac.start()
    load_source.start()

    barrier = pltpu.get_barrier_semaphore()

    def hello(row, theta, axial):
        pl.semaphore_signal(
            barrier, inc=1, device_id=(row, theta, axial), device_id_type=MESH
        )

    hello(y, t_next, a)
    hello(y, t_prev, a)
    pl.when(a > 0)(lambda: hello(y, t, a - 1))
    pl.when(a < nax - 1)(lambda: hello(y, t, a + 1))

    @pl.when(bnd)
    def _():
        def greet(i, carry):
            other = lax.rem(t + i, nth)
            mine = on_my_side(other)

            @pl.when(jnp.logical_and(i > 0, jnp.logical_or(owner, mine)))
            def _():
                hello(y, other, a)

            @pl.when(
                jnp.logical_and(
                    paired, jnp.logical_or(owner, jnp.logical_not(mine))
                )
            )
            def _():
                hello(py, other, pa)

            return carry

        lax.fori_loop(0, nth, greet, 0)

    lane1, lane16, sub16 = lanes(1), lanes(16), subs(16)

    def mode_column(slot):
        row = pack[slot, pl.ds(MODE_ROW, 1), :]
        picked = jnp.where(lane16 == sub16, jnp.broadcast_to(row, (16, 128)), 0.0)
        return jnp.sum(picked, axis=1, keepdims=True)

    def full_table(slot):
        column = mode_column(slot)
        wide = lax.broadcasted_iota(jnp.int32, (16, circle), 1).astype(F32)
        sn, cs = sin_cos(wide * column * (1.0 / circle))
        table = jnp.concatenate(
            [
                jnp.concatenate([cs, sn], axis=1),
                jnp.concatenate([-sn, cs], axis=1),
            ],
            axis=0,
        )
        hi = table.astype(BF16)
        lo = (table - hi.astype(F32)).astype(BF16)
        e_tab[slot] = jnp.concatenate([hi, lo, hi, jnp.zeros_like(hi)], axis=0)

    @pl.when(bnd)
    def _():
        mrow = jnp.zeros((1, 128), F32)
        for k in range(MODES):
            m_k = order[0, k].astype(F32) - (circle // 2)
            mrow = jnp.where(lax.rem(lane1, MODES) == k, m_k, mrow)
        pack[0, pl.ds(MODE_ROW, 1), :] = mrow
        slope = mrow * (2.0 / circle)
        sign = jnp.where(lax.rem(lane1, 2 * MODES) < MODES, -1.0, 1.0)
        for c in range(VARS):
            for w in range(VARS):
                i = c * VARS + w
                pack[0, pl.ds(i, 1), :] = (
                    giles[0, side, 0, 0, c, w] + slope * giles[0, side, 1, 0, c, w]
                )
                pack[0, pl.ds(25 + i, 1), :] = sign * (
                    giles[0, side, 0, 1, c, w] + slope * giles[0, side, 1, 1, c, w]
                )
                pack[0, pl.ds(50 + i, 1), :] = jnp.broadcast_to(
                    coupling[0, side, 0, c, w], (1, 128)
                )
                pack[0, pl.ds(75 + i, 1), :] = sign * coupling[0, side, 1, c, w]
        first_cell = (t * SECTOR).astype(F32)
        cell = first_cell + lax.rem(lane16, SECTOR).astype(F32)
        sn, cs = sin_cos(cell * mode_column(0) * (1.0 / circle))
        real = lax.rem(lane16, 2 * SECTOR) < SECTOR
        table = jnp.concatenate(
            [jnp.where(real, cs, sn), jnp.where(real, -sn, cs)], axis=0
        ) * (1.0 / circle)
        hi = high(table)
        lo = jnp.where(lanes(32) < 64, table - hi, 0.0)
        wf[...] = jnp.concatenate([hi, lo], axis=1).astype(BF16)
        rows = SECTOR + 16
        cell = first_cell - 8.0 + subs(rows).astype(F32)
        sn, cs = sin_cos(cell * mrow * (1.0 / circle))
        real = lax.rem(lanes(rows), 2 * MODES) < MODES
        table = jnp.concatenate(
            [jnp.where(real, cs, -sn), jnp.where(real, sn, cs)], axis=0
        )
        hi = high(table)
        lane = lanes(2 * rows)
        w2[...] = jnp.where(
            lane < 64, hi, jnp.where(lane < 96, table - hi, 0.0)
        ).astype(BF16)
        parts[pl.ds(320, 64), :] = jnp.zeros((64, 128), F32)

    pl.when(owner)(lambda: full_table(0))

    @pl.when(inlet)
    def _():
        for q in range(SECTIONS):
            v[q, :, :, 0, :, :] = jnp.zeros((2, VARS, 2 * PAD + SECTOR, 128), F32)

    @pl.when(outlet)
    def _():
        for q in range(SECTIONS):
            v[q, :, :, LAYERS + 1, :, :] = jnp.zeros(
                (2, VARS, 2 * PAD + SECTOR, 128), F32
            )

    pl.semaphore_wait(
        barrier,
        2
        + jnp.where(a > 0, 1, 0)
        + jnp.where(a < nax - 1, 1, 0)
        + jnp.where(
            bnd,
            jnp.where(owner, jnp.where(paired, 2 * nth - 1, nth - 1), nth),
            0,
        ),
    )

    def remote(src_ref, dst_ref, send, recv, device):
        return pltpu.make_async_remote_copy(
            src_ref=src_ref,
            dst_ref=dst_ref,
            send_sem=send,
            recv_sem=recv,
            device_id=device,
            device_id_type=MESH,
        )

    def theta_copies(q):
        return [
            remote(
                t_out.at[q, i], t_in.at[q, 1 - i], th_send.at[q, i],
                th_recv.at[q, 1 - i], (y, (t_prev, t_next)[i], a),
            )
            for i in range(2)
        ]

    def send_theta(q):
        def stage(i, carry):
            for p in range(2):
                for c in range(VARS):
                    t_out[q, 0, p, c, pl.ds(i, 1), :] = v[q, p, c, i + 1, FIRST : FIRST + 1, :]
                    t_out[q, 1, p, c, pl.ds(i, 1), :] = v[q, p, c, i + 1, LAST : LAST + 1, :]
            return carry

        lax.fori_loop(0, LAYERS, stage, 0)
        for copy in theta_copies(q):
            copy.start()

    def take_theta(q):
        for copy in theta_copies(q):
            copy.wait_recv()

        def place(i, carry):
            for p in range(2):
                for c in range(VARS):
                    v[q, p, c, i + 1, FIRST - 1 : FIRST, :] = t_in[q, 0, p, c, pl.ds(i, 1), :]
                    v[q, p, c, i + 1, LAST + 1 : LAST + 2, :] = t_in[q, 1, p, c, pl.ds(i, 1), :]
            return carry

        lax.fori_loop(0, LAYERS, place, 0)

    def axial_down(q):
        return remote(
            v.at[q, :, :, 1, OWN], v.at[q, :, :, LAYERS + 1, OWN],
            ax_send.at[q, 0], ax_recv.at[q, 1], (y, t, a - 1),
        )

    def axial_up(q):
        return remote(
            v.at[q, :, :, LAYERS, OWN], v.at[q, :, :, 0, OWN],
            ax_send.at[q, 1], ax_recv.at[q, 0], (y, t, a + 1),
        )

    def send_axial(q):
        pl.when(a > 0)(lambda: axial_down(q).start())
        pl.when(a < nax - 1)(lambda: axial_up(q).start())

    def take_axial(q):
        pl.when(a > 0)(lambda: wait_for(v.at[q, :, :, 0, OWN], ax_recv.at[q, 0]))
        pl.when(a < nax - 1)(
            lambda: wait_for(v.at[q, :, :, LAYERS + 1, OWN], ax_recv.at[q, 1])
        )

    frequency = blade[0].astype(F32) * OMEGA_UNIT
    lane8 = lanes(8)

    def stencil(q, first, last):
        weight = 1.0 / (SECTIONS - q)

        def layer(l, carry):
            for half in range(2):
                bases = [PAD + 16 * half, PAD + 16 * half + 8]
                acc = {}

                def add(key, value):
                    acc[key] = acc[key] + value if key in acc else value

                for w in range(VARS):
                    deltas = {}
                    for ti, base in enumerate(bases):
                        for p in range(2):
                            mid = v[q, p, w, l, base : base + 8, :]
                            tp = v[q, p, w, l, base + 1 : base + 9, :]
                            tm = v[q, p, w, l, base - 1 : base + 7, :]
                            ap = v[q, p, w, l + 1, base : base + 8, :]
                            am = v[q, p, w, l - 1, base : base + 8, :]
                            rp = jnp.where(lane8 == 127, 0.0, pltpu.roll(mid, 127, 1))
                            rm = jnp.where(lane8 == 0, 0.0, pltpu.roll(mid, 1, 1))
                            deltas[0, p, ti] = ap - am
                            deltas[1, p, ti] = tp - tm
                            deltas[2, p, ti] = rp - rm
                            total = (ap + am) + (tp + tm) + (rp + rm)
                            add((p, w, ti), DISSIPATION * total - 6 * DISSIPATION * mid)
                            turn = frequency * mid
                            add((1 - p, w, ti), turn if p == 1 else -turn)
                    for d in range(3):
                        for c in range(VARS):
                            jac = jb[(d * VARS + w) * VARS + c, l - 1]
                            for ti in range(2):
                                for p in range(2):
                                    add((p, c, ti), jac * deltas[d, p, ti])
                for ti, base in enumerate(bases):
                    here = dt[l - 1, base : base + 8, :] * weight
                    for p in range(2):
                        for c in range(VARS):
                            forced = (
                                src[p, c, l - 1, base - PAD : base - PAD + 8, :]
                                + acc[p, c, ti]
                            )
                            v[q + 1, p, c, l, base : base + 8, :] = (
                                v[0, p, c, l, base : base + 8, :] + here * forced
                            )
            return carry

        lax.fori_loop(first, last, layer, 0)

    def forward(q, group):
        blocks = []
        for c in range(VARS):
            blocks.append(
                jnp.concatenate(
                    [v[q, p, c, edge, PAD : PAD + SECTOR, :] for p in range(2)], axis=0
                )
            )
        x = jnp.concatenate(blocks, axis=1)
        hi = x.astype(BF16)
        lo = (x - hi.astype(F32)).astype(BF16)
        rhs = jnp.concatenate([hi, lo, hi, jnp.zeros_like(hi)], axis=0)
        res = jnp.dot(wf[...], rhs, preferred_element_type=F32)
        for c in range(VARS):
            parts[pl.ds(32 * (group + c), 32), :] = res[:, 128 * c : 128 * (c + 1)]

    def send_parts(rd):
        for u in range(3):
            block = parts[pl.ds(128 * u, 128), :].T
            sent[rd, :, :, 128 * u : 128 * (u + 1)] = block.reshape(nth, BAND, 128)

        def one(i, carry):
            band = lax.rem(t + i, nth)
            mine = on_my_side(band)
            own = jnp.logical_and(mine, i == 0)

            @pl.when(own)
            def _():
                pltpu.make_async_copy(
                    sent.at[rd, band], got.at[rd, t], p_recv.at[rd, 0]
                ).start()

            @pl.when(jnp.logical_not(own))
            def _():
                remote(
                    sent.at[rd, band],
                    got.at[rd, jnp.where(mine, t, nth + t)],
                    p_send.at[rd],
                    p_recv.at[rd, jnp.where(mine, 0, 1)],
                    (jnp.where(mine, y, py), band, jnp.where(mine, a, pa)),
                ).start()

            return carry

        lax.fori_loop(0, nth, one, 0)

    def swapped(x):
        return jnp.where(lane8 < MODES, pltpu.roll(x, 128 - MODES, 1), pltpu.roll(x, MODES, 1))

    def mixed(slot, coeffs, neighbour):
        turned = [swapped(x) for x in coeffs]
        turned_n = [swapped(x) for x in neighbour]
        result = []
        for c in range(VARS):
            total = jnp.zeros((8, 128), F32)
            for w in range(VARS):
                i = c * VARS + w
                total = total + pack[slot, pl.ds(i, 1), :] * coeffs[w]
                total = total + pack[slot, pl.ds(25 + i, 1), :] * turned[w]
                total = total + pack[slot, pl.ds(50 + i, 1), :] * neighbour[w]
                total = total + pack[slot, pl.ds(75 + i, 1), :] * turned_n[w]
            result.append(jnp.where(lane8 < 2 * MODES, total, 0.0))
        return result

    def response(slot, coeffs):
        blocks = []
        for x in coeffs:
            hi = high(x)
            blocks.append(hi + pltpu.roll(hi, 32, 1) + pltpu.roll(x - hi, 64, 1))
        lhs = jnp.concatenate(blocks + [blocks[0]], axis=0).astype(BF16)
        fix = jnp.dot(lhs, e_tab[slot], preferred_element_type=F32)
        cells = dt_all[slot]
        cells = jnp.concatenate([cells, cells], axis=1)
        fix = fix * jnp.concatenate([cells] * (VARS + 1), axis=0)
        hi = fix.astype(BF16)
        lo = (fix - hi.astype(F32)).astype(BF16)
        res = lax.dot_general(
            jnp.concatenate([hi, lo], axis=0),
            e_tab[slot],
            (((1,), (1,)), ((), ())),
            preferred_element_type=F32,
        )
        half = BAND * (VARS + 1)
        result = []
        for c in range(VARS):
            top = res[BAND * c : BAND * (c + 1)]
            low = res[half + BAND * c : half + BAND * (c + 1)]
            result.append(top + pltpu.roll(top, 96, 1) + low)
        return result

    def serve(rd):
        q = 2 * rd
        wait_for(got.at[rd, pl.ds(0, nth)], p_recv.at[rd, 0])
        pl.when(paired)(
            lambda: wait_for(got.at[rd, pl.ds(nth, nth)], p_recv.at[rd, 1])
        )
        groups = []
        for slot in range(2):
            total = got[rd, slot * nth]
            for i in range(1, nth):
                total = total + got[rd, slot * nth + i]
            pieces = []
            for g in range(2 * VARS):
                piece = total[:, 128 * (g // 4) : 128 * (g // 4 + 1)]
                if g % 4:
                    piece = pltpu.roll(piece, 128 - 32 * (g % 4), 1)
                if slot == 1:
                    piece = jnp.where(paired, piece, 0.0)
                pieces.append(piece)
            groups.append((pieces[:VARS], pieces[VARS:]))
            if rd == 0:
                for u in range(nth // 4):
                    cells = jnp.zeros((8, 128), F32)
                    for i in range(4):
                        tile = got[rd, slot * nth + 4 * u + i, :, 256:384]
                        if i != 2:
                            tile = pltpu.roll(tile, (32 * i + 64) % 128, 1)
                        cells = jnp.where(lane8 // 32 == i, tile, cells)
                    dt_all[slot, :, 128 * u : 128 * (u + 1)] = cells
        (own_now, own_next), (nbr_now, nbr_next) = groups
        c_own = mixed(0, own_now, nbr_now)
        c_nbr = mixed(1, nbr_now, own_now)
        scale = 1.0 / (SECTIONS - q) / circle
        own_next = [x - scale * r for x, r in zip(own_next, response(0, c_own))]
        nbr_next = [
            jnp.where(paired, x - scale * r, 0.0)
            for x, r in zip(nbr_next, response(1, c_nbr))
        ]
        d_own = mixed(0, own_next, nbr_next)
        d_nbr = mixed(1, nbr_next, own_next)
        for slot, values in ((0, c_own + d_own), (1, c_nbr + d_nbr)):
            for u in range(3):
                total = jnp.zeros((8, 128), F32)
                for i, x in enumerate(values[4 * u : 4 * u + 4]):
                    total = total + (pltpu.roll(x, 32 * i, 1) if i else x)
                c_out[rd, slot, :, 128 * u : 128 * (u + 1)] = total

        def one(i, carry):
            theta = lax.rem(t + i, nth)

            @pl.when(i == 0)
            def _():
                pltpu.make_async_copy(
                    c_out.at[rd, 0], c_in.at[rd, t], c_recv.at[rd]
                ).start()

            @pl.when(i > 0)
            def _():
                remote(
                    c_out.at[rd, 0], c_in.at[rd, t], c_send.at[rd], c_recv.at[rd],
                    (y, theta, a),
                ).start()

            @pl.when(paired)
            def _():
                remote(
                    c_out.at[rd, 1], c_in.at[rd, t], c_send.at[rd], c_recv.at[rd],
                    (py, theta, pa),
                ).start()

            return carry

        lax.fori_loop(0, nth, one, 0)

    def fixes(rd):
        wait_for(c_in.at[rd], c_recv.at[rd])
        rows = []
        for u in range(3):
            block = c_in[rd, :, :, 128 * u : 128 * (u + 1)].reshape(RADII, 128).T
            rows.extend(block[32 * i : 32 * (i + 1)] for i in range(4))
        result = []
        for s in range(2):
            x = jnp.concatenate(rows[VARS * s : VARS * (s + 1)], axis=1)
            hi = x.astype(BF16)
            lo = (x - hi.astype(F32)).astype(BF16)
            rhs = jnp.concatenate([hi, lo, hi, jnp.zeros_like(hi)], axis=0)
            result.append(jnp.dot(w2[...], rhs, preferred_element_type=F32))
        return result

    def subtract(q, fix, margin):
        weight = 1.0 / (SECTIONS - q)
        rows = SECTOR + 2 * margin
        base = PAD - margin
        here = dt[edge - 1, base : base + rows, :] * weight
        for p in range(2):
            for c in range(VARS):
                top = 48 * p + 8 - margin
                v[q + 1, p, c, edge, base : base + rows, :] = (
                    v[q + 1, p, c, edge, base : base + rows, :]
                    - here * fix[top : top + rows, 128 * c : 128 * (c + 1)]
                )

    load_state.wait()
    send_theta(0)
    send_axial(0)
    load_step.wait()

    def dt_copies():
        return [
            remote(
                dt.at[edge - 1, pl.ds(PAD, 8)], dt.at[edge - 1, pl.ds(PAD + SECTOR, 8)],
                dt_send.at[0], dt_recv.at[0], (y, t_prev, a),
            ),
            remote(
                dt.at[edge - 1, pl.ds(PAD + SECTOR - 8, 8)], dt.at[edge - 1, pl.ds(PAD - 8, 8)],
                dt_send.at[1], dt_recv.at[1], (y, t_next, a),
            ),
        ]

    def pack_copy():
        return remote(pack.at[0], pack.at[1], pk_sem.at[0], pk_sem.at[1], (py, t, pa))

    helps = jnp.logical_and(bnd, jnp.logical_not(owner))
    served = jnp.logical_and(owner, paired)

    @pl.when(bnd)
    def _():
        for copy in dt_copies():
            copy.start()
        pl.when(helps)(lambda: pack_copy().start())
        parts[pl.ds(320, 32), :] = dt[edge - 1, PAD : PAD + SECTOR, :]
        forward(0, 0)

    load_jac.wait()

    def spread(l, carry):
        for d in range(3):
            for w in range(VARS):
                for c in range(VARS):
                    jb[(d * VARS + w) * VARS + c, l] = jnp.broadcast_to(
                        jin[d, w, c, pl.ds(l, 1), :] * 0.5, (8, 128)
                    )
        return carry

    lax.fori_loop(0, LAYERS, spread, 0)
    load_source.wait()

    rest = (jnp.where(inlet, 2, 1), jnp.where(outlet, LAYERS, LAYERS + 1))
    far = (jnp.where(inlet, 3, 1), jnp.where(outlet, LAYERS - 1, LAYERS + 1))
    near = jnp.where(inlet, 1, LAYERS - 1)

    def result_copy(start, count):
        return pltpu.make_async_copy(
            v.at[SECTIONS, :, :, pl.ds(start, count), OWN],
            out.at[0, :, :, pl.ds(start - 1, count)],
            out_sem,
        )

    for rd in range(2):
        q = 2 * rd
        take_theta(q)

        @pl.when(bnd)
        def _():
            stencil(q, edge, edge + 1)
            if rd:
                forward(q, 0)
            forward(q + 1, VARS)
            send_parts(rd)

        take_axial(q)
        stencil(q, *rest)
        send_theta(q + 1)
        send_axial(q + 1)

        if rd == 0:

            @pl.when(served)
            def _():
                pack_copy().wait_recv()
                full_table(1)

        pl.when(owner)(lambda: serve(rd))
        take_theta(q + 1)
        take_axial(q + 1)
        stencil(q + 1, *far)
        if rd == 0:
            send_axial(q + 2)
        else:
            pl.when(inner)(lambda: result_copy(1, LAYERS).start())
            pl.when(bnd)(lambda: result_copy(far[0], LAYERS - 2).start())

        @pl.when(bnd)
        def _():
            if rd == 0:
                for copy in dt_copies():
                    copy.wait_recv()
            now, later = fixes(rd)
            subtract(q, now, 8)
            stencil(q + 1, near, near + 2)
            subtract(q + 1, later, 0)
            if rd:
                result_copy(near, 2).start()

        if rd == 0:
            send_theta(q + 2)

    for q in range(SECTIONS):
        for copy in theta_copies(q):
            copy.wait_send()
        pl.when(a > 0)(lambda: axial_down(q).wait_send())
        pl.when(a < nax - 1)(lambda: axial_up(q).wait_send())

    @pl.when(bnd)
    def _():
        for copy in dt_copies():
            copy.wait_send()
        pl.when(helps)(lambda: pack_copy().wait_send())
        for rd in range(2):
            pl.when(owner)(
                lambda: wait_for(sent.at[rd, pl.ds(0, nth - 1)], p_send.at[rd])
            )
            pl.when(helps)(lambda: wait_for(sent.at[rd], p_send.at[rd]))
            pl.when(served)(
                lambda: wait_for(got.at[rd, pl.ds(0, 2 * nth - 1)], c_send.at[rd])
            )
            pl.when(jnp.logical_and(owner, alone))(
                lambda: wait_for(got.at[rd, pl.ds(0, nth - 1)], c_send.at[rd])
            )

    wait_for(v.at[SECTIONS, :, :, pl.ds(1, LAYERS), OWN], out_sem)


def solution(mesh):
    nrow, nth, nax = mesh.shape["row"], mesh.shape["theta"], mesh.shape["axial"]

    def step(state, source, time_step, jacobian, blade, order, giles, coupling):
        circle = order.shape[1]
        cells = (2, VARS)
        anyspace = pl.BlockSpec(memory_space=pl.ANY)
        scalars = pl.BlockSpec(memory_space=pltpu.SMEM)
        dma = pltpu.SemaphoreType.DMA
        return pl.pallas_call(
            functools.partial(kernel, (nrow, nth, nax, circle)),
            out_shape=jax.ShapeDtypeStruct(state.shape, F32),
            in_specs=[anyspace] * 4 + [scalars] * 4,
            out_specs=anyspace,
            scratch_shapes=[
                pltpu.VMEM((SECTIONS + 1, *cells, LAYERS + 2, 2 * PAD + SECTOR, RADII), F32),
                pltpu.VMEM((*cells, LAYERS, SECTOR, RADII), F32),
                pltpu.VMEM((LAYERS, 2 * PAD + SECTOR, RADII), F32),
                pltpu.VMEM((3, VARS, VARS, LAYERS, RADII), F32),
                pltpu.VMEM((75, LAYERS, 8, RADII), F32),
                pltpu.VMEM((SECTIONS, 2, *cells, LAYERS, RADII), F32),
                pltpu.VMEM((SECTIONS, 2, *cells, LAYERS, RADII), F32),
                pltpu.VMEM((32, 256), BF16),
                pltpu.VMEM((2 * (SECTOR + 16), 128), BF16),
                pltpu.VMEM((2, 128, 2 * circle), BF16),
                pltpu.VMEM((2, 104, 128), F32),
                pltpu.VMEM((WIDE, 128), F32),
                pltpu.VMEM((2, nth, BAND, WIDE), F32),
                pltpu.VMEM((2, 2 * nth, BAND, WIDE), F32),
                pltpu.VMEM((2, BAND, circle), F32),
                pltpu.VMEM((2, 2, BAND, WIDE), F32),
                pltpu.VMEM((2, nth, BAND, WIDE), F32),
                dma((4,)),
                dma((SECTIONS, 2)),
                dma((SECTIONS, 2)),
                dma((SECTIONS, 2)),
                dma((SECTIONS, 2)),
                dma((2,)),
                dma((2,)),
                dma((2,)),
                dma((2,)),
                dma((2, 2)),
                dma((2,)),
                dma((2,)),
                dma,
            ],
            compiler_params=pltpu.CompilerParams(
                collective_id=0, has_side_effects=True, vmem_limit_bytes=48 * 2**20
            ),
        )(state, source, time_step, jacobian, blade, order, giles, coupling)

    return jax.shard_map(
        step,
        mesh=mesh,
        in_specs=(
            P("row", None, None, "axial", "theta", None),
            P("row", None, None, "axial", "theta", None),
            P("row", "axial", "theta", None),
            P("row", None, None, None, "axial", None),
            P("row"),
            P("row", None),
            P("row", None, None, None, None, None),
            P("row", None, None, None, None),
        ),
        out_specs=P("row", None, None, "axial", "theta", None),
        check_vma=False,
    )
```

```python
import functools
import math

import jax
import jax.numpy as jnp
from jax import lax
from jax.experimental import pallas as pl
from jax.experimental.pallas import tpu as pltpu
from jax.sharding import PartitionSpec as P

MESH = pl.DeviceIdType.MESH
F32 = jnp.float32
BF16 = jnp.bfloat16
MODES = 16
SECTIONS = 4
DISSIPATION = 0.05
OMEGA_UNIT = 0.02
LAYERS = 8
SECTOR = 32
RADII = 128
VARS = 5
PAD = 16
FIRST, LAST = PAD, PAD + SECTOR - 1
OWN = pl.ds(PAD, SECTOR)
BAND = 8
WIDE = 384
MODE_ROW = 100
VMEM_LIMIT = 48 * 2**20


def sin_cos(turns):
    h = (turns - jnp.floor(turns + 0.5)) * math.pi
    z = h * h
    s = 1.0 / 6227020800
    for d in (-39916800, 362880, -5040, 120, -6, 1):
        s = s * z + 1.0 / d
    s = s * h
    c = 1.0 / 479001600
    for d in (-3628800, 40320, -720, 24, -2, 1):
        c = c * z + 1.0 / d
    return 2.0 * s * c, 1.0 - 2.0 * s * s


def high(x):
    return x.astype(BF16).astype(F32)


def lanes(rows):
    return lax.broadcasted_iota(jnp.int32, (rows, 128), 1)


def subs(rows):
    return lax.broadcasted_iota(jnp.int32, (rows, 128), 0)


def wait_for(ref, sem):
    pltpu.make_async_copy(ref, ref, sem).wait()


def kernel(
    shape,
    state_in,
    source_in,
    step_in,
    jac_in,
    order,
    giles,
    coupling,
    blade,
    out,
    v,
    src,
    src_edge,
    dt,
    jin,
    jb,
    t_out,
    t_in,
    wf,
    w2,
    e_tab,
    pack,
    parts,
    sent,
    got,
    dt_all,
    c_out,
    c_in,
    load_sem,
    th_send,
    th_recv,
    ax_send,
    ax_recv,
    edge_send,
    edge_recv,
    tile_send,
    tile_recv,
    pk_sem,
    p_send,
    p_recv,
    c_send,
    c_recv,
):
    nrow, nth, nax, circle = shape
    y, t, a = lax.axis_index("row"), lax.axis_index("theta"), lax.axis_index("axial")
    inlet, outlet = a == 0, a == nax - 1
    bnd = jnp.logical_or(inlet, outlet)
    side = jnp.where(inlet, 0, 1)
    paired = jnp.logical_or(
        jnp.logical_and(inlet, y > 0), jnp.logical_and(outlet, y < nrow - 1)
    )
    alone = jnp.logical_not(paired)
    py = jnp.where(paired, jnp.where(inlet, y - 1, y + 1), y)
    pa = jnp.where(paired, jnp.where(inlet, nax - 1, 0), a)
    edge = jnp.where(inlet, 1, LAYERS)

    def on_my_side(band):
        return jnp.logical_or(alone, lax.rem(band // 2, 2) == side)

    owner = jnp.logical_and(bnd, on_my_side(t))
    nz = nth // 2

    def far_first(i):
        step = i // 2
        away = (step + 1) // 2
        dz = nz // 2 + jnp.where(lax.rem(step, 2) == 0, away, -away)
        return 2 * lax.rem(t // 2 + dz, nz) + lax.rem(i, 2)

    t_next, t_prev = lax.rem(t + 1, nth), lax.rem(t + nth - 1, nth)

    load_state = pltpu.make_async_copy(
        state_in.at[0], v.at[0, :, :, pl.ds(1, LAYERS), OWN], load_sem.at[0]
    )
    load_step = pltpu.make_async_copy(step_in.at[0], dt.at[:, OWN], load_sem.at[1])
    load_jac = pltpu.make_async_copy(jac_in.at[0], jin, load_sem.at[2])
    load_source = pltpu.make_async_copy(source_in.at[0], src, load_sem.at[3])
    load_state.start()
    load_step.start()
    load_jac.start()
    load_source.start()

    barrier = pltpu.get_barrier_semaphore()

    def hello(row, theta, axial):
        pl.semaphore_signal(
            barrier, inc=1, device_id=(row, theta, axial), device_id_type=MESH
        )

    hello(y, t_next, a)
    hello(y, t_prev, a)
    pl.when(a > 0)(lambda: hello(y, t, a - 1))
    pl.when(a < nax - 1)(lambda: hello(y, t, a + 1))

    @pl.when(bnd)
    def _():
        def greet(i, carry):
            other = far_first(i)
            mine = on_my_side(other)

            @pl.when(jnp.logical_and(other != t, jnp.logical_or(owner, mine)))
            def _():
                hello(y, other, a)

            @pl.when(
                jnp.logical_and(
                    paired, jnp.logical_or(owner, jnp.logical_not(mine))
                )
            )
            def _():
                hello(py, other, pa)

            return carry

        lax.fori_loop(0, nth, greet, 0)

    lane1, lane16, sub16 = lanes(1), lanes(16), subs(16)

    def mode_column(slot):
        row = pack[slot, pl.ds(MODE_ROW, 1), :]
        picked = jnp.where(lane16 == sub16, jnp.broadcast_to(row, (16, 128)), 0.0)
        return jnp.sum(picked, axis=1, keepdims=True)

    def full_table(slot):
        column = mode_column(slot)
        wide = lax.broadcasted_iota(jnp.int32, (16, circle), 1).astype(F32)
        sn, cs = sin_cos(wide * column * (1.0 / circle))
        table = jnp.concatenate(
            [
                jnp.concatenate([cs, sn], axis=1),
                jnp.concatenate([-sn, cs], axis=1),
            ],
            axis=0,
        )
        hi = table.astype(BF16)
        lo = (table - hi.astype(F32)).astype(BF16)
        e_tab[slot] = jnp.concatenate([hi, lo, hi, jnp.zeros_like(hi)], axis=0)

    @pl.when(bnd)
    def _():
        mrow = jnp.zeros((1, 128), F32)
        for k in range(MODES):
            m_k = order[0, k].astype(F32) - (circle // 2)
            mrow = jnp.where(lax.rem(lane1, MODES) == k, m_k, mrow)
        pack[0, pl.ds(MODE_ROW, 1), :] = mrow
        slope = mrow * (2.0 / circle)
        sign = jnp.where(lax.rem(lane1, 2 * MODES) < MODES, -1.0, 1.0)
        for c in range(VARS):
            for w in range(VARS):
                i = c * VARS + w
                pack[0, pl.ds(i, 1), :] = (
                    giles[0, side, 0, c, 0, w] + slope * giles[0, side, 1, c, 0, w]
                )
                pack[0, pl.ds(25 + i, 1), :] = sign * (
                    giles[0, side, 0, c, 1, w] + slope * giles[0, side, 1, c, 1, w]
                )
                pack[0, pl.ds(50 + i, 1), :] = jnp.broadcast_to(
                    coupling[0, side, c, 0, w], (1, 128)
                )
                pack[0, pl.ds(75 + i, 1), :] = sign * coupling[0, side, c, 1, w]
        first_cell = (t * SECTOR).astype(F32)
        cell = first_cell + lax.rem(lane16, SECTOR).astype(F32)
        sn, cs = sin_cos(cell * mode_column(0) * (1.0 / circle))
        real = lax.rem(lane16, 2 * SECTOR) < SECTOR
        table = jnp.concatenate(
            [jnp.where(real, cs, sn), jnp.where(real, -sn, cs)], axis=0
        ) * (1.0 / circle)
        hi = high(table)
        lo = jnp.where(lanes(32) < 64, table - hi, 0.0)
        wf[...] = jnp.concatenate([hi, lo], axis=1).astype(BF16)
        rows = SECTOR + 16
        cell = first_cell - 8.0 + subs(rows).astype(F32)
        sn, cs = sin_cos(cell * mrow * (1.0 / circle))
        real = lax.rem(lanes(rows), 2 * MODES) < MODES
        table = jnp.concatenate(
            [jnp.where(real, cs, -sn), jnp.where(real, sn, cs)], axis=0
        )
        hi = high(table)
        lane = lanes(2 * rows)
        w2[...] = jnp.where(
            lane < 64, hi, jnp.where(lane < 96, table - hi, 0.0)
        ).astype(BF16)
        parts[pl.ds(320, 64), :] = jnp.zeros((64, 128), F32)

    pl.when(owner)(lambda: full_table(0))

    @pl.when(inlet)
    def _():
        for q in range(SECTIONS):
            v[q, :, :, 0, :, :] = jnp.zeros((2, VARS, 2 * PAD + SECTOR, 128), F32)

    @pl.when(outlet)
    def _():
        for q in range(SECTIONS):
            v[q, :, :, LAYERS + 1, :, :] = jnp.zeros(
                (2, VARS, 2 * PAD + SECTOR, 128), F32
            )

    pl.semaphore_wait(
        barrier,
        2
        + jnp.where(a > 0, 1, 0)
        + jnp.where(a < nax - 1, 1, 0)
        + jnp.where(
            bnd,
            jnp.where(owner, jnp.where(paired, 2 * nth - 1, nth - 1), nth),
            0,
        ),
    )

    rest = (jnp.where(inlet, 2, 1), jnp.where(outlet, LAYERS, LAYERS + 1))

    def remote(src_ref, dst_ref, send, recv, device):
        return pltpu.make_async_remote_copy(
            src_ref=src_ref,
            dst_ref=dst_ref,
            send_sem=send,
            recv_sem=recv,
            device_id=device,
            device_id_type=MESH,
        )

    def theta_copies(q):
        return [
            remote(
                t_out.at[q, i], t_in.at[q, 1 - i], th_send.at[q, i],
                th_recv.at[q, 1 - i], (y, (t_prev, t_next)[i], a),
            )
            for i in range(2)
        ]

    def send_theta(q):
        def stage(i, carry):
            for p in range(2):
                for c in range(VARS):
                    t_out[q, 0, p, c, pl.ds(i, 1), :] = v[q, p, c, i + 1, FIRST : FIRST + 1, :]
                    t_out[q, 1, p, c, pl.ds(i, 1), :] = v[q, p, c, i + 1, LAST : LAST + 1, :]
            return carry

        lax.fori_loop(0, LAYERS, stage, 0)
        for copy in theta_copies(q):
            copy.start()

    def take_theta(q):
        for copy in theta_copies(q):
            copy.wait_recv()

        def place(i, carry):
            for p in range(2):
                for c in range(VARS):
                    v[q, p, c, i + 1, FIRST - 1 : FIRST, :] = t_in[q, 0, p, c, pl.ds(i, 1), :]
                    v[q, p, c, i + 1, LAST + 1 : LAST + 2, :] = t_in[q, 1, p, c, pl.ds(i, 1), :]
            return carry

        if q < SECTIONS - 1:
            lax.fori_loop(rest[0] - 1, rest[1] - 1, place, 0)
        else:
            lax.fori_loop(0, LAYERS, place, 0)

    def axial_down(q):
        return remote(
            v.at[q, :, :, 1, OWN], v.at[q, :, :, LAYERS + 1, OWN],
            ax_send.at[q, 0], ax_recv.at[q, 1], (y, t, a - 1),
        )

    def axial_up(q):
        return remote(
            v.at[q, :, :, LAYERS, OWN], v.at[q, :, :, 0, OWN],
            ax_send.at[q, 1], ax_recv.at[q, 0], (y, t, a + 1),
        )

    def send_axial(q):
        pl.when(a > 0)(lambda: axial_down(q).start())
        pl.when(a < nax - 1)(lambda: axial_up(q).start())

    def take_axial(q):
        pl.when(a > 0)(lambda: wait_for(v.at[q, :, :, 0, OWN], ax_recv.at[q, 0]))
        pl.when(a < nax - 1)(
            lambda: wait_for(v.at[q, :, :, LAYERS + 1, OWN], ax_recv.at[q, 1])
        )

    frequency = blade[0].astype(F32) * OMEGA_UNIT
    lane8 = lanes(8)

    def forcing(p, c, l, base):
        if base < PAD:
            return src_edge[0, p, c]
        if base >= PAD + SECTOR:
            return src_edge[1, p, c]
        return src[p, c, l - 1, base - PAD : base - PAD + 8, :]

    def tile_pair(q, l, first_row):
        weight = 1.0 / (SECTIONS - q)
        bases = [first_row, first_row + 8]
        acc = {}

        def add(key, value):
            acc[key] = acc[key] + value if key in acc else value

        for w in range(VARS):
            deltas = {}
            for ti, base in enumerate(bases):
                for p in range(2):
                    mid = v[q, p, w, l, base : base + 8, :]
                    tp = v[q, p, w, l, base + 1 : base + 9, :]
                    tm = v[q, p, w, l, base - 1 : base + 7, :]
                    ap = v[q, p, w, l + 1, base : base + 8, :]
                    am = v[q, p, w, l - 1, base : base + 8, :]
                    rp = jnp.where(lane8 == 127, 0.0, pltpu.roll(mid, 127, 1))
                    rm = jnp.where(lane8 == 0, 0.0, pltpu.roll(mid, 1, 1))
                    deltas[0, p, ti] = ap - am
                    deltas[1, p, ti] = tp - tm
                    deltas[2, p, ti] = rp - rm
                    total = (ap + am) + (tp + tm) + (rp + rm)
                    add((p, w, ti), DISSIPATION * total - 6 * DISSIPATION * mid)
                    turn = frequency * mid
                    add((1 - p, w, ti), turn if p == 1 else -turn)
            for d in range(3):
                for c in range(VARS):
                    jac = jb[(d * VARS + w) * VARS + c, l - 1]
                    for ti in range(2):
                        for p in range(2):
                            add((p, c, ti), jac * deltas[d, p, ti])
        for ti, base in enumerate(bases):
            here = dt[l - 1, base : base + 8, :] * weight
            for p in range(2):
                for c in range(VARS):
                    forced = (
                        forcing(p, c, l, base)
                        + acc[p, c, ti]
                    )
                    value = v[0, p, c, l, base : base + 8, :] + here * forced
                    if q == SECTIONS - 1:
                        out[0, p, c, l - 1, base - PAD : base - PAD + 8, :] = value
                    else:
                        v[q + 1, p, c, l, base : base + 8, :] = value

    def stencil(q, first, last):
        def layer(l, carry):
            for half in range(2):
                tile_pair(q, l, PAD + 16 * half)
            return carry

        lax.fori_loop(first, last, layer, 0)

    def forward(q, group):
        blocks = []
        for c in range(VARS):
            blocks.append(
                jnp.concatenate(
                    [v[q, p, c, edge, PAD : PAD + SECTOR, :] for p in range(2)], axis=0
                )
            )
        x = jnp.concatenate(blocks, axis=1)
        hi = x.astype(BF16)
        lo = (x - hi.astype(F32)).astype(BF16)
        rhs = jnp.concatenate([hi, lo, hi, jnp.zeros_like(hi)], axis=0)
        res = jnp.dot(wf[...], rhs, preferred_element_type=F32)
        for c in range(VARS):
            parts[pl.ds(32 * (group + c), 32), :] = res[:, 128 * c : 128 * (c + 1)]

    def send_parts(rd):
        for u in range(3):
            block = parts[pl.ds(128 * u, 128), :].T
            sent[rd, :, :, 128 * u : 128 * (u + 1)] = block.reshape(nth, BAND, 128)

        def one(i, carry):
            band = far_first(i)
            mine = on_my_side(band)
            own = jnp.logical_and(mine, band == t)

            @pl.when(own)
            def _():
                pltpu.make_async_copy(
                    sent.at[rd, band], got.at[rd, t], p_recv.at[rd, 0]
                ).start()

            @pl.when(jnp.logical_not(own))
            def _():
                remote(
                    sent.at[rd, band],
                    got.at[rd, jnp.where(mine, t, nth + t)],
                    p_send.at[rd],
                    p_recv.at[rd, jnp.where(mine, 0, 1)],
                    (jnp.where(mine, y, py), band, jnp.where(mine, a, pa)),
                ).start()

            return carry

        lax.fori_loop(0, nth, one, 0)

    def swapped(x):
        return jnp.where(lane8 < MODES, pltpu.roll(x, 128 - MODES, 1), pltpu.roll(x, MODES, 1))

    def mixed(slot, coeffs, neighbour):
        turned = [swapped(x) for x in coeffs]
        turned_n = [swapped(x) for x in neighbour]
        result = []
        for c in range(VARS):
            total = jnp.zeros((8, 128), F32)
            for w in range(VARS):
                i = c * VARS + w
                total = total + pack[slot, pl.ds(i, 1), :] * coeffs[w]
                total = total + pack[slot, pl.ds(25 + i, 1), :] * turned[w]
                total = total + pack[slot, pl.ds(50 + i, 1), :] * neighbour[w]
                total = total + pack[slot, pl.ds(75 + i, 1), :] * turned_n[w]
            result.append(jnp.where(lane8 < 2 * MODES, total, 0.0))
        return result

    def response(slot, coeffs):
        blocks = []
        for x in coeffs:
            hi = high(x)
            blocks.append(hi + pltpu.roll(hi, 32, 1) + pltpu.roll(x - hi, 64, 1))
        lhs = jnp.concatenate(blocks + [blocks[0]], axis=0).astype(BF16)
        fix = jnp.dot(lhs, e_tab[slot], preferred_element_type=F32)
        cells = dt_all[slot]
        cells = jnp.concatenate([cells, cells], axis=1)
        fix = fix * jnp.concatenate([cells] * (VARS + 1), axis=0)
        hi = fix.astype(BF16)
        lo = (fix - hi.astype(F32)).astype(BF16)
        res = lax.dot_general(
            jnp.concatenate([hi, lo], axis=0),
            e_tab[slot],
            (((1,), (1,)), ((), ())),
            preferred_element_type=F32,
        )
        half = BAND * (VARS + 1)
        result = []
        for c in range(VARS):
            top = res[BAND * c : BAND * (c + 1)]
            low = res[half + BAND * c : half + BAND * (c + 1)]
            result.append(top + pltpu.roll(top, 96, 1) + low)
        return result

    def serve(rd):
        q = 2 * rd
        wait_for(got.at[rd, pl.ds(0, nth)], p_recv.at[rd, 0])
        pl.when(paired)(
            lambda: wait_for(got.at[rd, pl.ds(nth, nth)], p_recv.at[rd, 1])
        )
        groups = []
        for slot in range(2):
            total = got[rd, slot * nth]
            for i in range(1, nth):
                total = total + got[rd, slot * nth + i]
            pieces = []
            for g in range(2 * VARS):
                piece = total[:, 128 * (g // 4) : 128 * (g // 4 + 1)]
                if g % 4:
                    piece = pltpu.roll(piece, 128 - 32 * (g % 4), 1)
                if slot == 1:
                    piece = jnp.where(paired, piece, 0.0)
                pieces.append(piece)
            groups.append((pieces[:VARS], pieces[VARS:]))
            if rd == 0:
                for u in range(nth // 4):
                    cells = jnp.zeros((8, 128), F32)
                    for i in range(4):
                        tile = got[rd, slot * nth + 4 * u + i, :, 256:384]
                        if i != 2:
                            tile = pltpu.roll(tile, (32 * i + 64) % 128, 1)
                        cells = jnp.where(lane8 // 32 == i, tile, cells)
                    dt_all[slot, :, 128 * u : 128 * (u + 1)] = cells
        (own_now, own_next), (nbr_now, nbr_next) = groups
        c_own = mixed(0, own_now, nbr_now)
        c_nbr = mixed(1, nbr_now, own_now)
        scale = 1.0 / (SECTIONS - q) / circle
        own_next = [x - scale * r for x, r in zip(own_next, response(0, c_own))]
        nbr_next = [
            jnp.where(paired, x - scale * r, 0.0)
            for x, r in zip(nbr_next, response(1, c_nbr))
        ]
        d_own = mixed(0, own_next, nbr_next)
        d_nbr = mixed(1, nbr_next, own_next)
        for slot, values in ((0, c_own + d_own), (1, c_nbr + d_nbr)):
            for u in range(3):
                total = jnp.zeros((8, 128), F32)
                for i, x in enumerate(values[4 * u : 4 * u + 4]):
                    total = total + (pltpu.roll(x, 32 * i, 1) if i else x)
                c_out[rd, slot, :, 128 * u : 128 * (u + 1)] = total

        def one(i, carry):
            theta = far_first(i)

            @pl.when(paired)
            def _():
                remote(
                    c_out.at[rd, 1], c_in.at[rd, t], c_send.at[rd], c_recv.at[rd],
                    (py, theta, pa),
                ).start()

            @pl.when(theta != t)
            def _():
                remote(
                    c_out.at[rd, 0], c_in.at[rd, t], c_send.at[rd], c_recv.at[rd],
                    (y, theta, a),
                ).start()

            @pl.when(theta == t)
            def _():
                pltpu.make_async_copy(
                    c_out.at[rd, 0], c_in.at[rd, t], c_recv.at[rd]
                ).start()

            return carry

        lax.fori_loop(0, nth, one, 0)

    def fixes(rd):
        wait_for(c_in.at[rd], c_recv.at[rd])
        rows = []
        for u in range(3):
            block = c_in[rd, :, :, 128 * u : 128 * (u + 1)].reshape(RADII, 128).T
            rows.extend(block[32 * i : 32 * (i + 1)] for i in range(4))
        result = []
        for s in range(2):
            x = jnp.concatenate(rows[VARS * s : VARS * (s + 1)], axis=1)
            hi = x.astype(BF16)
            lo = (x - hi.astype(F32)).astype(BF16)
            rhs = jnp.concatenate([hi, lo, hi, jnp.zeros_like(hi)], axis=0)
            result.append(jnp.dot(w2[...], rhs, preferred_element_type=F32))
        return result

    def subtract(q, fix, margin):
        weight = 1.0 / (SECTIONS - q)
        rows = SECTOR + 2 * margin
        base = PAD - margin
        here = dt[edge - 1, base : base + rows, :] * weight
        for p in range(2):
            for c in range(VARS):
                top = 48 * p + 8 - margin
                less = here * fix[top : top + rows, 128 * c : 128 * (c + 1)]
                if q == SECTIONS - 1:
                    out[0, p, c, edge - 1] = out[0, p, c, edge - 1] - less
                else:
                    v[q + 1, p, c, edge, base : base + rows, :] = (
                        v[q + 1, p, c, edge, base : base + rows, :] - less
                    )

    def edge_copies():
        plane = edge - 1
        copies = []
        for i, (at_, row, device) in enumerate(
            ((0, PAD + SECTOR, t_prev), (SECTOR - 8, PAD - 8, t_next))
        ):
            rows, place, device = pl.ds(at_, 8), pl.ds(row, 8), (y, device, a)
            copies += [
                remote(
                    state_in.at[0, :, :, plane, rows], v.at[0, :, :, edge, place],
                    edge_send.at[0, i], edge_recv.at[0, i], device,
                ),
                remote(
                    step_in.at[0, plane, rows], dt.at[plane, place],
                    edge_send.at[1, i], edge_recv.at[1, i], device,
                ),
                remote(
                    source_in.at[0, :, :, plane, rows], src_edge.at[1 - i],
                    edge_send.at[2, i], edge_recv.at[2, i], device,
                ),
            ]
        return copies

    def tile_copies():
        return [
            remote(
                v.at[1, :, :, edge, pl.ds(at_, 8)], v.at[1, :, :, edge, pl.ds(row, 8)],
                tile_send.at[i], tile_recv.at[i], (y, device, a),
            )
            for i, (at_, row, device) in enumerate(
                ((PAD, PAD + SECTOR, t_prev), (PAD + SECTOR - 8, PAD - 8, t_next))
            )
        ]

    def pack_copy():
        return remote(pack.at[0], pack.at[1], pk_sem.at[0], pk_sem.at[1], (py, t, pa))

    helps = jnp.logical_and(bnd, jnp.logical_not(owner))
    served = jnp.logical_and(owner, paired)

    @pl.when(bnd)
    def _():
        for copy in edge_copies():
            copy.start()
        pl.when(helps)(lambda: pack_copy().start())

    load_state.wait()
    send_theta(0)
    send_axial(0)
    load_step.wait()

    @pl.when(bnd)
    def _():
        parts[pl.ds(320, 32), :] = dt[edge - 1, PAD : PAD + SECTOR, :]
        forward(0, 0)

    load_jac.wait()

    def spread(l, carry):
        for d in range(3):
            for w in range(VARS):
                for c in range(VARS):
                    jb[(d * VARS + w) * VARS + c, l] = jnp.broadcast_to(
                        jin[d, w, c, pl.ds(l, 1), :] * 0.5, (8, 128)
                    )
        return carry

    lax.fori_loop(0, LAYERS, spread, 0)
    load_source.wait()

    far = (jnp.where(inlet, 3, 1), jnp.where(outlet, LAYERS - 1, LAYERS + 1))
    near = jnp.where(inlet, 1, LAYERS - 1)
    second = jnp.where(inlet, 2, LAYERS - 1)

    for rd in range(2):
        q = 2 * rd

        @pl.when(bnd)
        def _():
            if rd == 0:
                for copy in edge_copies():
                    copy.wait_recv()
            for half in range(2):
                tile_pair(q, edge, PAD + 16 * half)
            if rd:
                forward(q, 0)
            forward(q + 1, VARS)
            send_parts(rd)
            if rd == 0:
                for copy in tile_copies():
                    copy.start()

        take_theta(q)
        take_axial(q)
        stencil(q, *rest)
        send_theta(q + 1)
        send_axial(q + 1)

        if rd == 0:

            @pl.when(served)
            def _():
                pack_copy().wait_recv()
                full_table(1)

        pl.when(owner)(lambda: serve(rd))
        take_theta(q + 1)
        take_axial(q + 1)
        stencil(q + 1, *far)
        if rd == 0:
            send_axial(q + 2)

        @pl.when(bnd)
        def _():
            now, later = fixes(rd)
            if rd == 0:
                for copy in tile_copies():
                    copy.wait()
                subtract(q, now, 8)
                for third in range(3):
                    tile_pair(q + 1, edge, PAD - 8 + 16 * third)
                stencil(q + 1, second, second + 1)
                subtract(q + 1, later, 8)
            else:
                subtract(q, now, 8)
                stencil(q + 1, near, near + 2)
                subtract(q + 1, later, 0)

        if rd == 0:
            send_theta(q + 2)

    for q in range(SECTIONS):
        for copy in theta_copies(q):
            copy.wait_send()
        pl.when(a > 0)(lambda: axial_down(q).wait_send())
        pl.when(a < nax - 1)(lambda: axial_up(q).wait_send())

    @pl.when(bnd)
    def _():
        for copy in edge_copies():
            copy.wait_send()
        pl.when(helps)(lambda: pack_copy().wait_send())
        for rd in range(2):
            pl.when(owner)(
                lambda: wait_for(sent.at[rd, pl.ds(0, nth - 1)], p_send.at[rd])
            )
            pl.when(helps)(lambda: wait_for(sent.at[rd], p_send.at[rd]))
            pl.when(served)(
                lambda: wait_for(got.at[rd, pl.ds(0, 2 * nth - 1)], c_send.at[rd])
            )
            pl.when(jnp.logical_and(owner, alone))(
                lambda: wait_for(got.at[rd, pl.ds(0, nth - 1)], c_send.at[rd])
            )


def solution(mesh):
    nrow, nth, nax = mesh.shape["row"], mesh.shape["theta"], mesh.shape["axial"]

    def step(state, source, time_step, jacobian, blade, order, giles, coupling):
        circle = order.shape[1]
        giles = giles.transpose(0, 1, 2, 4, 3, 5)
        coupling = coupling.transpose(0, 1, 3, 2, 4)
        cells = (2, VARS)
        anyspace = pl.BlockSpec(memory_space=pl.ANY)
        scalars = pl.BlockSpec(memory_space=pltpu.SMEM)
        dma = pltpu.SemaphoreType.DMA
        return pl.pallas_call(
            functools.partial(kernel, (nrow, nth, nax, circle)),
            out_shape=pltpu.VMEM(state.shape, F32),
            in_specs=[anyspace] * 4 + [scalars] * 4,
            out_specs=pl.BlockSpec(memory_space=pltpu.VMEM),
            scratch_shapes=[
                pltpu.VMEM((SECTIONS, *cells, LAYERS + 2, 2 * PAD + SECTOR, RADII), F32),
                pltpu.VMEM((*cells, LAYERS, SECTOR, RADII), F32),
                pltpu.VMEM((2, *cells, 8, RADII), F32),
                pltpu.VMEM((LAYERS, 2 * PAD + SECTOR, RADII), F32),
                pltpu.VMEM((3, VARS, VARS, LAYERS, RADII), F32),
                pltpu.VMEM((75, LAYERS, 8, RADII), F32),
                pltpu.VMEM((SECTIONS, 2, *cells, LAYERS, RADII), F32),
                pltpu.VMEM((SECTIONS, 2, *cells, LAYERS, RADII), F32),
                pltpu.VMEM((32, 256), BF16),
                pltpu.VMEM((2 * (SECTOR + 16), 128), BF16),
                pltpu.VMEM((2, 128, 2 * circle), BF16),
                pltpu.VMEM((2, 104, 128), F32),
                pltpu.VMEM((WIDE, 128), F32),
                pltpu.VMEM((2, nth, BAND, WIDE), F32),
                pltpu.VMEM((2, 2 * nth, BAND, WIDE), F32),
                pltpu.VMEM((2, BAND, circle), F32),
                pltpu.VMEM((2, 2, BAND, WIDE), F32),
                pltpu.VMEM((2, nth, BAND, WIDE), F32),
                dma((4,)),
                dma((SECTIONS, 2)),
                dma((SECTIONS, 2)),
                dma((SECTIONS, 2)),
                dma((SECTIONS, 2)),
                dma((3, 2)),
                dma((3, 2)),
                dma((2,)),
                dma((2,)),
                dma((2,)),
                dma((2,)),
                dma((2, 2)),
                dma((2,)),
                dma((2,)),
            ],
            compiler_params=pltpu.CompilerParams(
                collective_id=0, has_side_effects=True, vmem_limit_bytes=VMEM_LIMIT
            ),
        )(
            *(
                pltpu.with_memory_space_constraint(x, pltpu.HBM)
                for x in (state, source, time_step, jacobian, order, giles, coupling)
            ),
            blade,
        )

    return jax.shard_map(
        step,
        mesh=mesh,
        in_specs=(
            P("row", None, None, "axial", "theta", None),
            P("row", None, None, "axial", "theta", None),
            P("row", "axial", "theta", None),
            P("row", None, None, None, "axial", None),
            P("row"),
            P("row", None),
            P("row", None, None, None, None, None),
            P("row", None, None, None, None),
        ),
        out_specs=P("row", None, None, "axial", "theta", None),
        check_vma=False,
    )
```

```python
import functools
import math

import jax
import jax.numpy as jnp
from jax import lax
from jax.experimental import pallas as pl
from jax.experimental.pallas import tpu as pltpu
from jax.sharding import PartitionSpec as P

MESH = pl.DeviceIdType.MESH
F32 = jnp.float32
BF16 = jnp.bfloat16
MODES = 16
SECTIONS = 4
DISSIPATION = 0.05
OMEGA_UNIT = 0.02
LAYERS = 8
SECTOR = 32
RADII = 128
VARS = 5
PAD = 16
FIRST, LAST = PAD, PAD + SECTOR - 1
OWN = pl.ds(PAD, SECTOR)
BAND = 8
MODE_ROW = 100
VMEM_LIMIT = 48 * 2**20


def sin_cos(turns):
    h = (turns - jnp.floor(turns + 0.5)) * math.pi
    z = h * h
    s = 1.0 / 6227020800
    for d in (-39916800, 362880, -5040, 120, -6, 1):
        s = s * z + 1.0 / d
    s = s * h
    c = 1.0 / 479001600
    for d in (-3628800, 40320, -720, 24, -2, 1):
        c = c * z + 1.0 / d
    return 2.0 * s * c, 1.0 - 2.0 * s * s


def high(x):
    return x.astype(BF16).astype(F32)


def lanes(rows):
    return lax.broadcasted_iota(jnp.int32, (rows, 128), 1)


def subs(rows):
    return lax.broadcasted_iota(jnp.int32, (rows, 128), 0)


def wait_for(ref, sem):
    pltpu.make_async_copy(ref, ref, sem).wait()


def kernel(
    shape,
    state_in,
    source_in,
    step_in,
    jac_in,
    order_in,
    giles_in,
    coupling_in,
    blade,
    out,
    order,
    giles,
    coupling,
    v,
    src,
    src_edge,
    dt,
    jin,
    jb,
    t_out,
    t_in,
    wf,
    w2,
    e_tab,
    pack,
    parts,
    sent,
    sent_x,
    got,
    got_x,
    got_dt,
    dt_all,
    c_out,
    c_out_x,
    c_in,
    c_in_x,
    spare,
    load_sem,
    th_send,
    th_recv,
    ax_send,
    ax_recv,
    edge_send,
    edge_recv,
    tile_send,
    tile_recv,
    pk_sem,
    p_send,
    p_recv,
    x_send,
    x_recv,
    c_send,
    c_recv,
    y_send,
    y_recv,
):
    nrow, nth, nax, circle = shape
    y, t, a = lax.axis_index("row"), lax.axis_index("theta"), lax.axis_index("axial")
    inlet, outlet = a == 0, a == nax - 1
    bnd = jnp.logical_or(inlet, outlet)
    side = jnp.where(inlet, 0, 1)
    paired = jnp.logical_or(
        jnp.logical_and(inlet, y > 0), jnp.logical_and(outlet, y < nrow - 1)
    )
    alone = jnp.logical_not(paired)
    py = jnp.where(paired, jnp.where(inlet, y - 1, y + 1), y)
    pa = jnp.where(paired, jnp.where(inlet, nax - 1, 0), a)
    edge = jnp.where(inlet, 1, LAYERS)

    def on_my_side(band):
        return jnp.logical_or(alone, lax.rem(band // 2, 2) == side)

    owner = jnp.logical_and(bnd, on_my_side(t))
    nz = nth // 2

    def far_first(i):
        step = i // 2
        away = (step + 1) // 2
        dz = nz // 2 + jnp.where(lax.rem(step, 2) == 0, away, -away)
        return 2 * lax.rem(t // 2 + dz, nz) + lax.rem(i, 2)

    t_next, t_prev = lax.rem(t + 1, nth), lax.rem(t + nth - 1, nth)

    load_state = pltpu.make_async_copy(
        state_in.at[0], v.at[0, :, :, pl.ds(1, LAYERS), OWN], load_sem.at[0]
    )
    load_step = pltpu.make_async_copy(step_in.at[0], dt.at[:, OWN], load_sem.at[1])
    load_jac = pltpu.make_async_copy(jac_in.at[0], jin, load_sem.at[2])
    load_source = pltpu.make_async_copy(source_in.at[0], src, load_sem.at[3])
    load_small = [
        pltpu.make_async_copy(order_in, order, load_sem.at[4]),
        pltpu.make_async_copy(giles_in, giles, load_sem.at[5]),
        pltpu.make_async_copy(coupling_in, coupling, load_sem.at[6]),
    ]
    load_state.start()

    barrier = pltpu.get_barrier_semaphore()

    def hello(row, theta, axial):
        pl.semaphore_signal(
            barrier, inc=1, device_id=(row, theta, axial), device_id_type=MESH
        )

    hello(y, t_next, a)
    hello(y, t_prev, a)
    pl.when(a > 0)(lambda: hello(y, t, a - 1))
    pl.when(a < nax - 1)(lambda: hello(y, t, a + 1))

    @pl.when(bnd)
    def _():
        def greet(i, carry):
            other = far_first(i)
            mine = on_my_side(other)

            @pl.when(jnp.logical_and(other != t, jnp.logical_or(owner, mine)))
            def _():
                hello(y, other, a)

            @pl.when(
                jnp.logical_and(
                    paired, jnp.logical_or(owner, jnp.logical_not(mine))
                )
            )
            def _():
                hello(py, other, pa)

            return carry

        lax.fori_loop(0, nth, greet, 0)

    load_step.start()

    @pl.when(bnd)
    def _():
        for copy in load_small:
            copy.start()

    load_jac.start()
    load_source.start()

    lane1, lane16, sub16 = lanes(1), lanes(16), subs(16)

    def mode_column(slot):
        row = pack[slot, pl.ds(MODE_ROW, 1), :]
        picked = jnp.where(lane16 == sub16, jnp.broadcast_to(row, (16, 128)), 0.0)
        return jnp.sum(picked, axis=1, keepdims=True)

    def full_table(slot):
        column = mode_column(slot)
        wide = lax.broadcasted_iota(jnp.int32, (16, circle), 1).astype(F32)
        sn, cs = sin_cos(wide * column * (1.0 / circle))
        table = jnp.concatenate(
            [
                jnp.concatenate([cs, sn], axis=1),
                jnp.concatenate([-sn, cs], axis=1),
            ],
            axis=0,
        )
        hi = table.astype(BF16)
        lo = (table - hi.astype(F32)).astype(BF16)
        e_tab[slot] = jnp.concatenate([hi, lo, hi, jnp.zeros_like(hi)], axis=0)

    @pl.when(bnd)
    def _():
        for copy in load_small:
            copy.wait()
        mrow = jnp.zeros((1, 128), F32)
        for k in range(MODES):
            m_k = order[0, k].astype(F32) - (circle // 2)
            mrow = jnp.where(lax.rem(lane1, MODES) == k, m_k, mrow)
        pack[0, pl.ds(MODE_ROW, 1), :] = mrow
        slope = mrow * (2.0 / circle)
        sign = jnp.where(lax.rem(lane1, 2 * MODES) < MODES, -1.0, 1.0)
        for c in range(VARS):
            for w in range(VARS):
                i = c * VARS + w
                pack[0, pl.ds(i, 1), :] = (
                    giles[0, side, 0, c, 0, w] + slope * giles[0, side, 1, c, 0, w]
                )
                pack[0, pl.ds(25 + i, 1), :] = sign * (
                    giles[0, side, 0, c, 1, w] + slope * giles[0, side, 1, c, 1, w]
                )
                pack[0, pl.ds(50 + i, 1), :] = jnp.broadcast_to(
                    coupling[0, side, c, 0, w], (1, 128)
                )
                pack[0, pl.ds(75 + i, 1), :] = sign * coupling[0, side, c, 1, w]
        first_cell = (t * SECTOR).astype(F32)
        cell = first_cell + lax.rem(lane16, SECTOR).astype(F32)
        sn, cs = sin_cos(cell * mode_column(0) * (1.0 / circle))
        real = lax.rem(lane16, 2 * SECTOR) < SECTOR
        table = jnp.concatenate(
            [jnp.where(real, cs, sn), jnp.where(real, -sn, cs)], axis=0
        ) * (1.0 / circle)
        hi = high(table)
        lo = jnp.where(lanes(32) < 64, table - hi, 0.0)
        wf[...] = jnp.concatenate([hi, lo], axis=1).astype(BF16)
        rows = SECTOR + 16
        cell = first_cell - 8.0 + subs(rows).astype(F32)
        sn, cs = sin_cos(cell * mrow * (1.0 / circle))
        real = lax.rem(lanes(rows), 2 * MODES) < MODES
        table = jnp.concatenate(
            [jnp.where(real, cs, -sn), jnp.where(real, sn, cs)], axis=0
        )
        hi = high(table)
        lane = lanes(2 * rows)
        w2[...] = jnp.where(
            lane < 64, hi, jnp.where(lane < 96, table - hi, 0.0)
        ).astype(BF16)
        parts[pl.ds(160, 96), :] = jnp.zeros((96, 128), F32)

    pl.when(owner)(lambda: full_table(0))

    @pl.when(inlet)
    def _():
        for q in range(SECTIONS):
            v[q, :, :, 0, :, :] = jnp.zeros((2, VARS, 2 * PAD + SECTOR, 128), F32)

    @pl.when(outlet)
    def _():
        for q in range(SECTIONS):
            v[q, :, :, LAYERS + 1, :, :] = jnp.zeros(
                (2, VARS, 2 * PAD + SECTOR, 128), F32
            )

    pl.semaphore_wait(
        barrier,
        2
        + jnp.where(a > 0, 1, 0)
        + jnp.where(a < nax - 1, 1, 0)
        + jnp.where(
            bnd,
            jnp.where(owner, jnp.where(paired, 2 * nth - 1, nth - 1), nth),
            0,
        ),
    )

    def remote(src_ref, dst_ref, send, recv, device):
        return pltpu.make_async_remote_copy(
            src_ref=src_ref,
            dst_ref=dst_ref,
            send_sem=send,
            recv_sem=recv,
            device_id=device,
            device_id_type=MESH,
        )

    def theta_copies(q):
        return [
            remote(
                t_out.at[q, i], t_in.at[q, 1 - i], th_send.at[q, i],
                th_recv.at[q, 1 - i], (y, (t_prev, t_next)[i], a),
            )
            for i in range(2)
        ]

    def flat(q, p, c):
        return v.at[q, p, c].reshape((LAYERS + 2) * (2 * PAD + SECTOR), RADII)

    def column(row):
        return pl.ds(2 * PAD + SECTOR + row, LAYERS, stride=2 * PAD + SECTOR)

    def send_theta(q):
        for p in range(2):
            for c in range(VARS):
                rows = flat(q, p, c)
                t_out[q, 0, p, c] = rows[column(FIRST), :]
                t_out[q, 1, p, c] = rows[column(LAST), :]
        for copy in theta_copies(q):
            copy.start()

    def take_theta(q):
        for copy in theta_copies(q):
            copy.wait_recv()

        for p in range(2):
            for c in range(VARS):
                rows = flat(q, p, c)
                rows[column(FIRST - 1), :] = t_in[q, 0, p, c]
                rows[column(LAST + 1), :] = t_in[q, 1, p, c]

    def axial_down(q):
        return remote(
            v.at[q, :, :, 1, OWN], v.at[q, :, :, LAYERS + 1, OWN],
            ax_send.at[q, 0], ax_recv.at[q, 1], (y, t, a - 1),
        )

    def axial_up(q):
        return remote(
            v.at[q, :, :, LAYERS, OWN], v.at[q, :, :, 0, OWN],
            ax_send.at[q, 1], ax_recv.at[q, 0], (y, t, a + 1),
        )

    def send_axial(q):
        pl.when(a > 0)(lambda: axial_down(q).start())
        pl.when(a < nax - 1)(lambda: axial_up(q).start())

    def take_axial(q):
        pl.when(a > 0)(lambda: wait_for(v.at[q, :, :, 0, OWN], ax_recv.at[q, 0]))
        pl.when(a < nax - 1)(
            lambda: wait_for(v.at[q, :, :, LAYERS + 1, OWN], ax_recv.at[q, 1])
        )

    frequency = blade[0].astype(F32) * OMEGA_UNIT
    lane8 = lanes(8)

    def forcing(p, c, l, base):
        if base < PAD:
            return src_edge[0, p, c]
        if base >= PAD + SECTOR:
            return src_edge[1, p, c]
        return src[p, c, l - 1, base - PAD : base - PAD + 8, :]

    def tile_pair(q, l, bases):
        weight = 1.0 / (SECTIONS - q)
        acc = {}

        def add(key, value):
            acc[key] = acc[key] + value if key in acc else value

        for w in range(VARS):
            deltas = {}
            for ti, base in enumerate(bases):
                for p in range(2):
                    mid = v[q, p, w, l, base : base + 8, :]
                    tp = v[q, p, w, l, base + 1 : base + 9, :]
                    tm = v[q, p, w, l, base - 1 : base + 7, :]
                    ap = v[q, p, w, l + 1, base : base + 8, :]
                    am = v[q, p, w, l - 1, base : base + 8, :]
                    rp = jnp.where(lane8 == 127, 0.0, pltpu.roll(mid, 127, 1))
                    rm = jnp.where(lane8 == 0, 0.0, pltpu.roll(mid, 1, 1))
                    deltas[0, p, ti] = ap - am
                    deltas[1, p, ti] = tp - tm
                    deltas[2, p, ti] = rp - rm
                    total = (ap + am) + (tp + tm) + (rp + rm)
                    add((p, w, ti), DISSIPATION * total - 6 * DISSIPATION * mid)
                    turn = frequency * mid
                    add((1 - p, w, ti), turn if p == 1 else -turn)
            for d in range(3):
                for c in range(VARS):
                    jac = jb[(d * VARS + w) * VARS + c, l - 1]
                    for ti in range(2):
                        for p in range(2):
                            add((p, c, ti), jac * deltas[d, p, ti])
        for ti, base in enumerate(bases):
            here = dt[l - 1, base : base + 8, :] * weight
            for p in range(2):
                for c in range(VARS):
                    forced = (
                        forcing(p, c, l, base)
                        + acc[p, c, ti]
                    )
                    value = v[0, p, c, l, base : base + 8, :] + here * forced
                    if q == SECTIONS - 1:
                        out[0, p, c, l - 1, base - PAD : base - PAD + 8, :] = value
                    else:
                        v[q + 1, p, c, l, base : base + 8, :] = value

    middle, sides = (PAD + 8, PAD + 16), (PAD, PAD + 24)

    def stencil(q, first, last, *pairs):
        def layer(l, carry):
            for pair in pairs or (middle, sides):
                tile_pair(q, l, pair)
            return carry

        lax.fori_loop(first, last, layer, 0)

    def outer_layers(q):
        def layer(i, carry):
            for pair in (middle, sides):
                tile_pair(q, 1 + (LAYERS - 1) * i, pair)
            return carry

        lax.fori_loop(jnp.where(inlet, 1, 0), jnp.where(outlet, 1, 2), layer, 0)

    def forward(q):
        blocks = []
        for c in range(VARS):
            blocks.append(
                jnp.concatenate(
                    [v[q, p, c, edge, PAD : PAD + SECTOR, :] for p in range(2)], axis=0
                )
            )
        x = jnp.concatenate(blocks, axis=1)
        hi = x.astype(BF16)
        lo = (x - hi.astype(F32)).astype(BF16)
        rhs = jnp.concatenate([hi, lo, hi, jnp.zeros_like(hi)], axis=0)
        res = jnp.dot(wf[...], rhs, preferred_element_type=F32)
        for c in range(VARS):
            parts[pl.ds(32 * c, 32), :] = res[:, 128 * c : 128 * (c + 1)]

    def pack_rows(q, at_):
        total = jnp.zeros((32, 128), F32)
        for i in range(4):
            rows = spare[pl.ds(i, 32, stride=4), :]
            shift = (32 * i - at_) % 128
            rows = pltpu.roll(rows, shift, 1) if shift else rows
            total = jnp.where(lanes(32) // 32 == i, rows, total)
        for b in range(nth):
            sent_x[q, b] = total[2 * b : 2 * b + 2]

    def send_parts(q):
        sent[q] = parts[pl.ds(0, 128), :].T.reshape(nth, BAND, 128)
        spare[...] = parts[pl.ds(128, 128), :].T
        pack_rows(q, 0)
        if q == 0:
            pack_rows(SECTIONS, 32)

        def one(i, carry):
            band = far_first(i)
            mine = on_my_side(band)
            own = jnp.logical_and(mine, band == t)
            slot = jnp.where(mine, t, nth + t)
            which = jnp.where(mine, 0, 1)
            ways = [
                (sent.at[q, band], got.at[q, slot], p_send.at[q], p_recv.at[q, which]),
                (sent_x.at[q, band], got_x.at[q, slot], x_send.at[q], x_recv.at[q, which]),
            ]
            if q == 0:
                ways.append(
                    (
                        sent_x.at[SECTIONS, band], got_dt.at[slot],
                        x_send.at[SECTIONS], x_recv.at[SECTIONS, which],
                    )
                )

            @pl.when(own)
            def _():
                for here, there, _, recv in ways:
                    pltpu.make_async_copy(here, there, recv).start()

            @pl.when(jnp.logical_not(own))
            def _():
                device = (jnp.where(mine, y, py), band, jnp.where(mine, a, pa))
                for here, there, send, recv in ways:
                    remote(here, there, send, recv, device).start()

            return carry

        lax.fori_loop(0, nth, one, 0)

    def swapped(x):
        return jnp.where(lane8 < MODES, pltpu.roll(x, 128 - MODES, 1), pltpu.roll(x, MODES, 1))

    def mixed(slot, coeffs, neighbour):
        turned = [swapped(x) for x in coeffs]
        turned_n = [swapped(x) for x in neighbour]
        result = []
        for c in range(VARS):
            total = jnp.zeros((8, 128), F32)
            for w in range(VARS):
                i = c * VARS + w
                total = total + pack[slot, pl.ds(i, 1), :] * coeffs[w]
                total = total + pack[slot, pl.ds(25 + i, 1), :] * turned[w]
                total = total + pack[slot, pl.ds(50 + i, 1), :] * neighbour[w]
                total = total + pack[slot, pl.ds(75 + i, 1), :] * turned_n[w]
            result.append(jnp.where(lane8 < 2 * MODES, total, 0.0))
        return result

    def response(slot, coeffs):
        blocks = []
        for x in coeffs:
            hi = high(x)
            blocks.append(hi + pltpu.roll(hi, 32, 1) + pltpu.roll(x - hi, 64, 1))
        lhs = jnp.concatenate(blocks + [blocks[0]], axis=0).astype(BF16)
        fix = jnp.dot(lhs, e_tab[slot], preferred_element_type=F32)
        cells = dt_all[slot]
        cells = jnp.concatenate([cells, cells], axis=1)
        fix = fix * jnp.concatenate([cells] * (VARS + 1), axis=0)
        hi = fix.astype(BF16)
        lo = (fix - hi.astype(F32)).astype(BF16)
        res = lax.dot_general(
            jnp.concatenate([hi, lo], axis=0),
            e_tab[slot],
            (((1,), (1,)), ((), ())),
            preferred_element_type=F32,
        )
        half = BAND * (VARS + 1)
        result = []
        for c in range(VARS):
            top = res[BAND * c : BAND * (c + 1)]
            low = res[half + BAND * c : half + BAND * (c + 1)]
            result.append(top + pltpu.roll(top, 96, 1) + low)
        return result

    sub8 = subs(8)

    def unpacked(rows, at_=0):
        wide = jnp.where(sub8 < 4, rows[0:1], rows[1:2])
        result = wide
        for i in range(4):
            shift = (at_ - 32 * i) % 128
            turned = pltpu.roll(wide, shift, 1) if shift else wide
            result = jnp.where(lax.rem(sub8, 4) == i, turned, result)
        return result

    def packed(x):
        total = jnp.zeros((8, 128), F32)
        for i in range(4):
            turned = pltpu.roll(x, 32 * i, 1) if i else x
            total = jnp.where(lax.rem(sub8, 4) == i, turned, total)
        return jnp.concatenate(
            [
                jnp.sum(total[0:4], axis=0, keepdims=True),
                jnp.sum(total[4:8], axis=0, keepdims=True),
            ],
            axis=0,
        )

    def sums(q):
        def arrive(which):
            wait_for(got.at[q, pl.ds(which * nth, nth)], p_recv.at[q, which])
            wait_for(got_x.at[q, pl.ds(which * nth, nth)], x_recv.at[q, which])
            if q == 0:
                wait_for(
                    got_dt.at[pl.ds(which * nth, nth)], x_recv.at[SECTIONS, which]
                )

        arrive(0)
        pl.when(paired)(lambda: arrive(1))
        result = []
        for slot in range(2):
            total, last = got[q, slot * nth], got_x[q, slot * nth]
            for i in range(1, nth):
                total = total + got[q, slot * nth + i]
                last = last + got_x[q, slot * nth + i]
            pieces = [pltpu.roll(total, 128 - 32 * g, 1) if g else total for g in range(4)]
            pieces.append(unpacked(last))
            if slot == 1:
                pieces = [jnp.where(paired, x, 0.0) for x in pieces]
            result.append(pieces)
        return result

    def gather_steps():
        for slot in range(2):
            for u in range(nth // 4):
                cells = jnp.zeros((8, 128), F32)
                for i in range(4):
                    tile = unpacked(got_dt[slot * nth + 4 * u + i], 32 * i)
                    cells = jnp.where(lane8 // 32 == i, tile, cells)
                dt_all[slot, :, 128 * u : 128 * (u + 1)] = cells

    def send_modes(q, own, neighbour):
        for slot, values in ((0, own), (1, neighbour)):
            total = values[0]
            for i in range(1, 4):
                total = total + pltpu.roll(values[i], 32 * i, 1)
            c_out[q, slot] = total
            c_out_x[q, slot] = packed(values[4])

        def one(i, carry):
            theta = far_first(i)

            def send(slot, device):
                remote(
                    c_out.at[q, slot], c_in.at[q, t], c_send.at[q], c_recv.at[q], device
                ).start()
                remote(
                    c_out_x.at[q, slot], c_in_x.at[q, t], y_send.at[q], y_recv.at[q], device
                ).start()

            pl.when(paired)(lambda: send(1, (py, theta, pa)))
            pl.when(theta != t)(lambda: send(0, (y, theta, a)))

            @pl.when(theta == t)
            def _():
                pltpu.make_async_copy(
                    c_out.at[q, 0], c_in.at[q, t], c_recv.at[q]
                ).start()
                pltpu.make_async_copy(
                    c_out_x.at[q, 0], c_in_x.at[q, t], y_recv.at[q]
                ).start()

            return carry

        lax.fori_loop(0, nth, one, 0)

    def serve(q):
        own, nbr = sums(q)
        c_own = mixed(0, own, nbr)
        c_nbr = mixed(1, nbr, own)
        send_modes(q, c_own, c_nbr)
        if q == 0:
            gather_steps()
        scale = 1.0 / (SECTIONS - q) / circle
        r_own, r_nbr = response(0, c_own), response(1, c_nbr)
        own, nbr = sums(q + 1)
        own = [x - scale * r for x, r in zip(own, r_own)]
        nbr = [jnp.where(paired, x - scale * r, 0.0) for x, r in zip(nbr, r_nbr)]
        send_modes(q + 1, mixed(0, own, nbr), mixed(1, nbr, own))

    def fix_of(q):
        wait_for(c_in.at[q], c_recv.at[q])
        wait_for(c_in_x.at[q], y_recv.at[q])
        block = c_in[q].reshape(RADII, 128).T
        rows = [block[32 * i : 32 * (i + 1)] for i in range(4)]
        for b in range(nth):
            parts[pl.ds(2 * b, 2), :] = c_in_x[q, b]
        last = parts[pl.ds(0, 32), :]
        for i in range(4):
            spare[pl.ds(i, 32, stride=4), :] = (
                pltpu.roll(last, 128 - 32 * i, 1) if i else last
            )
        rows.append(spare[...].T[0:32])
        x = jnp.concatenate(rows, axis=1)
        hi = x.astype(BF16)
        lo = (x - hi.astype(F32)).astype(BF16)
        rhs = jnp.concatenate([hi, lo, hi, jnp.zeros_like(hi)], axis=0)
        return jnp.dot(w2[...], rhs, preferred_element_type=F32)

    def subtract(q, fix, margin):
        weight = 1.0 / (SECTIONS - q)
        rows = SECTOR + 2 * margin
        base = PAD - margin
        here = dt[edge - 1, base : base + rows, :] * weight
        for p in range(2):
            for c in range(VARS):
                top = 48 * p + 8 - margin
                less = here * fix[top : top + rows, 128 * c : 128 * (c + 1)]
                if q == SECTIONS - 1:
                    out[0, p, c, edge - 1] = out[0, p, c, edge - 1] - less
                else:
                    v[q + 1, p, c, edge, base : base + rows, :] = (
                        v[q + 1, p, c, edge, base : base + rows, :] - less
                    )

    def edge_copies():
        plane = edge - 1
        copies = []
        for i, (at_, row, device) in enumerate(
            ((0, PAD + SECTOR, t_prev), (SECTOR - 8, PAD - 8, t_next))
        ):
            rows, place, device = pl.ds(at_, 8), pl.ds(row, 8), (y, device, a)
            copies += [
                remote(
                    state_in.at[0, :, :, plane, rows], v.at[0, :, :, edge, place],
                    edge_send.at[0, i], edge_recv.at[0, i], device,
                ),
                remote(
                    step_in.at[0, plane, rows], dt.at[plane, place],
                    edge_send.at[1, i], edge_recv.at[1, i], device,
                ),
                remote(
                    source_in.at[0, :, :, plane, rows], src_edge.at[1 - i],
                    edge_send.at[2, i], edge_recv.at[2, i], device,
                ),
            ]
        return copies

    def plane_tile(i):
        return v.at[0, :, :, edge, pl.ds((PAD + SECTOR, PAD - 8)[i], 8)]

    def tile_copies():
        return [
            remote(
                v.at[1, :, :, edge, pl.ds(at_, 8)], v.at[1, :, :, edge, pl.ds(row, 8)],
                tile_send.at[i], tile_recv.at[i], (y, device, a),
            )
            for i, (at_, row, device) in enumerate(
                ((PAD, PAD + SECTOR, t_prev), (PAD + SECTOR - 8, PAD - 8, t_next))
            )
        ]

    def pack_copy():
        return remote(pack.at[0], pack.at[1], pk_sem.at[0], pk_sem.at[1], (py, t, pa))

    helps = jnp.logical_and(bnd, jnp.logical_not(owner))
    served = jnp.logical_and(owner, paired)

    @pl.when(bnd)
    def _():
        for copy in edge_copies():
            copy.start()
        pl.when(helps)(lambda: pack_copy().start())

    load_state.wait()
    send_theta(0)
    send_axial(0)
    load_step.wait()

    @pl.when(bnd)
    def _():
        parts[pl.ds(160, 32), :] = dt[edge - 1, PAD : PAD + SECTOR, :]
        forward(0)
        send_parts(0)

    load_jac.wait()

    def spread(l, carry):
        for d in range(3):
            for w in range(VARS):
                for c in range(VARS):
                    jb[(d * VARS + w) * VARS + c, l] = jnp.broadcast_to(
                        jin[d, w, c, pl.ds(l, 1), :] * 0.5, (8, 128)
                    )
        return carry

    lax.fori_loop(0, LAYERS, spread, 0)
    load_source.wait()

    far = (jnp.where(inlet, 3, 2), jnp.where(outlet, LAYERS - 1, LAYERS))
    near = jnp.where(inlet, 1, LAYERS - 1)
    second = jnp.where(inlet, 2, LAYERS - 1)

    for q in (0, 2):

        @pl.when(bnd)
        def _():
            if q == 0:
                for i in range(2):
                    wait_for(plane_tile(i), edge_recv.at[0, i])
            else:
                forward(q)
                send_parts(q)
            for pair in (middle, sides):
                tile_pair(q, edge, pair)
            forward(q + 1)
            send_parts(q + 1)
            if q == 0:
                for copy in tile_copies():
                    copy.start()

        if q:
            send_theta(q)
        stencil(q, 2, LAYERS, middle)
        take_theta(q)
        stencil(q, 2, LAYERS, sides)
        if q == 0:

            @pl.when(served)
            def _():
                pack_copy().wait_recv()
                full_table(1)

        take_axial(q)
        outer_layers(q)
        send_theta(q + 1)
        send_axial(q + 1)
        pl.when(owner)(lambda: serve(q))
        stencil(q + 1, *far, middle)
        if q == 0:

            @pl.when(bnd)
            def _():
                for copy in tile_copies():
                    copy.wait()

        take_theta(q + 1)
        stencil(q + 1, *far, sides)
        take_axial(q + 1)
        outer_layers(q + 1)
        if q == 0:
            send_axial(q + 2)

        @pl.when(bnd)
        def _():
            now = fix_of(q)
            if q == 0:
                for i in range(2):
                    wait_for(dt.at[edge - 1, pl.ds(PAD, 8)], edge_recv.at[1, i])
                    wait_for(src_edge.at[i], edge_recv.at[2, i])
                subtract(q, now, 8)
                for third in range(3):
                    first = PAD - 8 + 16 * third
                    tile_pair(q + 1, edge, (first, first + 8))
                stencil(q + 1, second, second + 1)
                subtract(q + 1, fix_of(q + 1), 8)
            else:
                subtract(q, now, 8)
                stencil(q + 1, near, near + 2)
                subtract(q + 1, fix_of(q + 1), 0)

    for q in range(SECTIONS):
        for copy in theta_copies(q):
            copy.wait_send()
        pl.when(a > 0)(lambda: axial_down(q).wait_send())
        pl.when(a < nax - 1)(lambda: axial_up(q).wait_send())

    @pl.when(bnd)
    def _():
        for copy in edge_copies():
            copy.wait_send()
        pl.when(helps)(lambda: pack_copy().wait_send())
        for q in range(SECTIONS):
            alike = ((sent, p_send, got, c_send), (sent_x, x_send, got_x, y_send))
            for mine, mine_sem, theirs, theirs_sem in alike:
                pl.when(owner)(
                    lambda: wait_for(mine.at[q, pl.ds(0, nth - 1)], mine_sem.at[q])
                )
                pl.when(helps)(lambda: wait_for(mine.at[q], mine_sem.at[q]))
                pl.when(served)(
                    lambda: wait_for(theirs.at[q, pl.ds(0, 2 * nth - 1)], theirs_sem.at[q])
                )
                pl.when(jnp.logical_and(owner, alone))(
                    lambda: wait_for(theirs.at[q, pl.ds(0, nth - 1)], theirs_sem.at[q])
                )
        pl.when(owner)(
            lambda: wait_for(
                sent_x.at[SECTIONS, pl.ds(0, nth - 1)], x_send.at[SECTIONS]
            )
        )
        pl.when(helps)(lambda: wait_for(sent_x.at[SECTIONS], x_send.at[SECTIONS]))


def solution(mesh):
    nrow, nth, nax = mesh.shape["row"], mesh.shape["theta"], mesh.shape["axial"]

    def step(state, source, time_step, jacobian, blade, order, giles, coupling):
        circle = order.shape[1]
        giles = giles.transpose(0, 1, 2, 4, 3, 5)
        coupling = coupling.transpose(0, 1, 3, 2, 4)
        cells = (2, VARS)
        anyspace = pl.BlockSpec(memory_space=pl.ANY)
        scalars = pl.BlockSpec(memory_space=pltpu.SMEM)
        dma = pltpu.SemaphoreType.DMA
        return pl.pallas_call(
            functools.partial(kernel, (nrow, nth, nax, circle)),
            out_shape=pltpu.VMEM(state.shape, F32),
            in_specs=[anyspace] * 7 + [scalars],
            out_specs=pl.BlockSpec(memory_space=pltpu.VMEM),
            scratch_shapes=[
                pltpu.SMEM(order.shape, jnp.int32),
                pltpu.SMEM(giles.shape, F32),
                pltpu.SMEM(coupling.shape, F32),
                pltpu.VMEM((SECTIONS, *cells, LAYERS + 2, 2 * PAD + SECTOR, RADII), F32),
                pltpu.VMEM((*cells, LAYERS, SECTOR, RADII), F32),
                pltpu.VMEM((2, *cells, 8, RADII), F32),
                pltpu.VMEM((LAYERS, 2 * PAD + SECTOR, RADII), F32),
                pltpu.VMEM((3, VARS, VARS, LAYERS, RADII), F32),
                pltpu.VMEM((75, LAYERS, 8, RADII), F32),
                pltpu.VMEM((SECTIONS, 2, *cells, LAYERS, RADII), F32),
                pltpu.VMEM((SECTIONS, 2, *cells, LAYERS, RADII), F32),
                pltpu.VMEM((32, 256), BF16),
                pltpu.VMEM((2 * (SECTOR + 16), 128), BF16),
                pltpu.VMEM((2, 128, 2 * circle), BF16),
                pltpu.VMEM((2, 104, 128), F32),
                pltpu.VMEM((256, 128), F32),
                pltpu.VMEM((SECTIONS, nth, BAND, 128), F32),
                pltpu.VMEM((SECTIONS + 1, nth, 2, 128), F32),
                pltpu.VMEM((SECTIONS, 2 * nth, BAND, 128), F32),
                pltpu.VMEM((SECTIONS, 2 * nth, 2, 128), F32),
                pltpu.VMEM((2 * nth, 2, 128), F32),
                pltpu.VMEM((2, BAND, circle), F32),
                pltpu.VMEM((SECTIONS, 2, BAND, 128), F32),
                pltpu.VMEM((SECTIONS, 2, 2, 128), F32),
                pltpu.VMEM((SECTIONS, nth, BAND, 128), F32),
                pltpu.VMEM((SECTIONS, nth, 2, 128), F32),
                pltpu.VMEM((RADII, 128), F32),
                dma((7,)),
                dma((SECTIONS, 2)),
                dma((SECTIONS, 2)),
                dma((SECTIONS, 2)),
                dma((SECTIONS, 2)),
                dma((3, 2)),
                dma((3, 2)),
                dma((2,)),
                dma((2,)),
                dma((2,)),
                dma((SECTIONS,)),
                dma((SECTIONS, 2)),
                dma((SECTIONS + 1,)),
                dma((SECTIONS + 1, 2)),
                dma((SECTIONS,)),
                dma((SECTIONS,)),
                dma((SECTIONS,)),
                dma((SECTIONS,)),
            ],
            compiler_params=pltpu.CompilerParams(
                collective_id=0, has_side_effects=True, vmem_limit_bytes=VMEM_LIMIT
            ),
        )(
            *(
                pltpu.with_memory_space_constraint(x, pltpu.HBM)
                for x in (state, source, time_step, jacobian, order, giles, coupling)
            ),
            blade,
        )

    return jax.shard_map(
        step,
        mesh=mesh,
        in_specs=(
            P("row", None, None, "axial", "theta", None),
            P("row", None, None, "axial", "theta", None),
            P("row", "axial", "theta", None),
            P("row", None, None, None, "axial", None),
            P("row"),
            P("row", None),
            P("row", None, None, None, None, None),
            P("row", None, None, None, None),
        ),
        out_specs=P("row", None, None, "axial", "theta", None),
        check_vma=False,
    )
```

```python
import functools
import math

import jax
import jax.numpy as jnp
from jax import lax
from jax.experimental import pallas as pl
from jax.experimental.pallas import tpu as pltpu
from jax.sharding import PartitionSpec as P

MESH = pl.DeviceIdType.MESH
F32 = jnp.float32
BF16 = jnp.bfloat16
MODES = 16
SECTIONS = 4
DISSIPATION = 0.05
OMEGA_UNIT = 0.02
LAYERS = 8
SECTOR = 32
RADII = 128
VARS = 5
PAD = 16
FIRST, LAST = PAD, PAD + SECTOR - 1
OWN = pl.ds(PAD, SECTOR)
BAND = 8
MODE_ROW = 100
VMEM_LIMIT = 48 * 2**20


def sin_cos(turns):
    h = (turns - jnp.floor(turns + 0.5)) * math.pi
    z = h * h
    s = 1.0 / 6227020800
    for d in (-39916800, 362880, -5040, 120, -6, 1):
        s = s * z + 1.0 / d
    s = s * h
    c = 1.0 / 479001600
    for d in (-3628800, 40320, -720, 24, -2, 1):
        c = c * z + 1.0 / d
    return 2.0 * s * c, 1.0 - 2.0 * s * s


def high(x):
    return x.astype(BF16).astype(F32)


def lanes(rows):
    return lax.broadcasted_iota(jnp.int32, (rows, 128), 1)


def subs(rows):
    return lax.broadcasted_iota(jnp.int32, (rows, 128), 0)


def wait_for(ref, sem):
    pltpu.make_async_copy(ref, ref, sem).wait()


def kernel(
    shape,
    state_in,
    source_in,
    step_in,
    jac_in,
    order_in,
    giles_in,
    coupling_in,
    blade,
    out,
    order,
    giles,
    coupling,
    v,
    src,
    src_edge,
    dt,
    jin,
    jb,
    t_out,
    t_in,
    wf,
    w2,
    e_tab,
    pack,
    parts,
    sent,
    sent_x,
    got,
    got_x,
    got_dt,
    dt_all,
    c_out,
    c_out_x,
    c_in,
    c_in_x,
    spare,
    load_sem,
    th_send,
    th_recv,
    ax_send,
    ax_recv,
    edge_send,
    edge_recv,
    tile_send,
    tile_recv,
    pk_sem,
    p_send,
    p_recv,
    x_send,
    x_recv,
    c_send,
    c_recv,
    y_send,
    y_recv,
):
    nrow, nth, nax, circle = shape
    y, t, a = lax.axis_index("row"), lax.axis_index("theta"), lax.axis_index("axial")
    inlet, outlet = a == 0, a == nax - 1
    bnd = jnp.logical_or(inlet, outlet)
    side = jnp.where(inlet, 0, 1)
    paired = jnp.logical_or(
        jnp.logical_and(inlet, y > 0), jnp.logical_and(outlet, y < nrow - 1)
    )
    alone = jnp.logical_not(paired)
    py = jnp.where(paired, jnp.where(inlet, y - 1, y + 1), y)
    pa = jnp.where(paired, jnp.where(inlet, nax - 1, 0), a)
    edge = jnp.where(inlet, 1, LAYERS)

    def on_my_side(band):
        return jnp.logical_or(alone, lax.rem(band // 2, 2) == side)

    owner = jnp.logical_and(bnd, on_my_side(t))
    nz = nth // 2

    def far_first(i):
        step = i // 2
        away = (step + 1) // 2
        dz = nz // 2 + jnp.where(lax.rem(step, 2) == 0, away, -away)
        return 2 * lax.rem(t // 2 + dz, nz) + lax.rem(i, 2)

    t_next, t_prev = lax.rem(t + 1, nth), lax.rem(t + nth - 1, nth)

    load_state = pltpu.make_async_copy(
        state_in.at[0], v.at[0, :, :, pl.ds(1, LAYERS), OWN], load_sem.at[0]
    )
    load_step = pltpu.make_async_copy(step_in.at[0], dt.at[:, OWN], load_sem.at[1])
    load_jac = pltpu.make_async_copy(jac_in.at[0], jin, load_sem.at[2])
    load_source = pltpu.make_async_copy(source_in.at[0], src, load_sem.at[3])
    load_small = [
        pltpu.make_async_copy(order_in, order, load_sem.at[4]),
        pltpu.make_async_copy(giles_in, giles, load_sem.at[5]),
        pltpu.make_async_copy(coupling_in, coupling, load_sem.at[6]),
    ]
    load_state.start()

    barrier = pltpu.get_barrier_semaphore()

    def hello(row, theta, axial):
        pl.semaphore_signal(
            barrier, inc=1, device_id=(row, theta, axial), device_id_type=MESH
        )

    hello(y, t_next, a)
    hello(y, t_prev, a)
    pl.when(a > 0)(lambda: hello(y, t, a - 1))
    pl.when(a < nax - 1)(lambda: hello(y, t, a + 1))

    @pl.when(bnd)
    def _():
        def greet(i, carry):
            other = far_first(i)
            mine = on_my_side(other)

            @pl.when(jnp.logical_and(other != t, jnp.logical_or(owner, mine)))
            def _():
                hello(y, other, a)

            @pl.when(
                jnp.logical_and(
                    paired, jnp.logical_or(owner, jnp.logical_not(mine))
                )
            )
            def _():
                hello(py, other, pa)

            return carry

        lax.fori_loop(0, nth, greet, 0)

    load_step.start()

    @pl.when(bnd)
    def _():
        for copy in load_small:
            copy.start()

    load_jac.start()
    load_source.start()

    lane1, lane16, sub16 = lanes(1), lanes(16), subs(16)

    def mode_column(slot):
        row = pack[slot, pl.ds(MODE_ROW, 1), :]
        picked = jnp.where(lane16 == sub16, jnp.broadcast_to(row, (16, 128)), 0.0)
        return jnp.sum(picked, axis=1, keepdims=True)

    def full_table(slot):
        column = mode_column(slot)
        wide = lax.broadcasted_iota(jnp.int32, (16, circle), 1).astype(F32)
        sn, cs = sin_cos(wide * column * (1.0 / circle))
        table = jnp.concatenate(
            [
                jnp.concatenate([cs, sn], axis=1),
                jnp.concatenate([-sn, cs], axis=1),
            ],
            axis=0,
        )
        hi = table.astype(BF16)
        lo = (table - hi.astype(F32)).astype(BF16)
        e_tab[slot] = jnp.concatenate([hi, lo, hi, jnp.zeros_like(hi)], axis=0)

    @pl.when(bnd)
    def _():
        for copy in load_small:
            copy.wait()
        mrow = jnp.zeros((1, 128), F32)
        for k in range(MODES):
            m_k = order[0, k].astype(F32) - (circle // 2)
            mrow = jnp.where(lax.rem(lane1, MODES) == k, m_k, mrow)
        pack[0, pl.ds(MODE_ROW, 1), :] = mrow
        slope = mrow * (2.0 / circle)
        sign = jnp.where(lax.rem(lane1, 2 * MODES) < MODES, -1.0, 1.0)
        for c in range(VARS):
            for w in range(VARS):
                i = c * VARS + w
                pack[0, pl.ds(i, 1), :] = (
                    giles[0, side, 0, c, 0, w] + slope * giles[0, side, 1, c, 0, w]
                )
                pack[0, pl.ds(25 + i, 1), :] = sign * (
                    giles[0, side, 0, c, 1, w] + slope * giles[0, side, 1, c, 1, w]
                )
                pack[0, pl.ds(50 + i, 1), :] = jnp.broadcast_to(
                    coupling[0, side, c, 0, w], (1, 128)
                )
                pack[0, pl.ds(75 + i, 1), :] = sign * coupling[0, side, c, 1, w]
        first_cell = (t * SECTOR).astype(F32)
        cell = first_cell + lax.rem(lane16, SECTOR).astype(F32)
        sn, cs = sin_cos(cell * mode_column(0) * (1.0 / circle))
        real = lax.rem(lane16, 2 * SECTOR) < SECTOR
        table = jnp.concatenate(
            [jnp.where(real, cs, sn), jnp.where(real, -sn, cs)], axis=0
        ) * (1.0 / circle)
        hi = high(table)
        lo = jnp.where(lanes(32) < 64, table - hi, 0.0)
        wf[...] = jnp.concatenate([hi, lo], axis=1).astype(BF16)
        rows = SECTOR + 16
        cell = first_cell - 8.0 + subs(rows).astype(F32)
        sn, cs = sin_cos(cell * mrow * (1.0 / circle))
        real = lax.rem(lanes(rows), 2 * MODES) < MODES
        table = jnp.concatenate(
            [jnp.where(real, cs, -sn), jnp.where(real, sn, cs)], axis=0
        )
        hi = high(table)
        lane = lanes(2 * rows)
        w2[...] = jnp.where(
            lane < 64, hi, jnp.where(lane < 96, table - hi, 0.0)
        ).astype(BF16)
        parts[pl.ds(160, 96), :] = jnp.zeros((96, 128), F32)

    pl.when(owner)(lambda: full_table(0))

    @pl.when(inlet)
    def _():
        for q in range(SECTIONS):
            v[q, :, :, 0, :, :] = jnp.zeros((2, VARS, 2 * PAD + SECTOR, 128), F32)

    @pl.when(outlet)
    def _():
        for q in range(SECTIONS):
            v[q, :, :, LAYERS + 1, :, :] = jnp.zeros(
                (2, VARS, 2 * PAD + SECTOR, 128), F32
            )

    def remote(src_ref, dst_ref, send, recv, device):
        return pltpu.make_async_remote_copy(
            src_ref=src_ref,
            dst_ref=dst_ref,
            send_sem=send,
            recv_sem=recv,
            device_id=device,
            device_id_type=MESH,
        )

    def theta_copies(q):
        return [
            remote(
                t_out.at[q, i], t_in.at[q, 1 - i], th_send.at[q, i],
                th_recv.at[q, 1 - i], (y, (t_prev, t_next)[i], a),
            )
            for i in range(2)
        ]

    def flat(q, p, c):
        return v.at[q, p, c].reshape((LAYERS + 2) * (2 * PAD + SECTOR), RADII)

    def column(row):
        return pl.ds(2 * PAD + SECTOR + row, LAYERS, stride=2 * PAD + SECTOR)

    def stage_theta(q):
        for p in range(2):
            for c in range(VARS):
                rows = flat(q, p, c)
                t_out[q, 0, p, c] = rows[column(FIRST), :]
                t_out[q, 1, p, c] = rows[column(LAST), :]

    def send_theta(q):
        stage_theta(q)
        for copy in theta_copies(q):
            copy.start()

    def take_theta(q):
        for copy in theta_copies(q):
            copy.wait_recv()

        for p in range(2):
            for c in range(VARS):
                rows = flat(q, p, c)
                rows[column(FIRST - 1), :] = t_in[q, 0, p, c]
                rows[column(LAST + 1), :] = t_in[q, 1, p, c]

    def axial_down(q):
        return remote(
            v.at[q, :, :, 1, OWN], v.at[q, :, :, LAYERS + 1, OWN],
            ax_send.at[q, 0], ax_recv.at[q, 1], (y, t, a - 1),
        )

    def axial_up(q):
        return remote(
            v.at[q, :, :, LAYERS, OWN], v.at[q, :, :, 0, OWN],
            ax_send.at[q, 1], ax_recv.at[q, 0], (y, t, a + 1),
        )

    def send_axial(q):
        pl.when(a > 0)(lambda: axial_down(q).start())
        pl.when(a < nax - 1)(lambda: axial_up(q).start())

    def take_axial(q):
        pl.when(a > 0)(lambda: wait_for(v.at[q, :, :, 0, OWN], ax_recv.at[q, 0]))
        pl.when(a < nax - 1)(
            lambda: wait_for(v.at[q, :, :, LAYERS + 1, OWN], ax_recv.at[q, 1])
        )

    frequency = blade[0].astype(F32) * OMEGA_UNIT
    lane8 = lanes(8)

    def forcing(p, c, l, base):
        if base < PAD:
            return src_edge[0, p, c]
        if base >= PAD + SECTOR:
            return src_edge[1, p, c]
        return src[p, c, l - 1, base - PAD : base - PAD + 8, :]

    def tile_pair(q, l, bases):
        weight = 1.0 / (SECTIONS - q)
        acc = {}

        def add(key, value):
            acc[key] = acc[key] + value if key in acc else value

        for w in range(VARS):
            deltas = {}
            for ti, base in enumerate(bases):
                for p in range(2):
                    mid = v[q, p, w, l, base : base + 8, :]
                    tp = v[q, p, w, l, base + 1 : base + 9, :]
                    tm = v[q, p, w, l, base - 1 : base + 7, :]
                    ap = v[q, p, w, l + 1, base : base + 8, :]
                    am = v[q, p, w, l - 1, base : base + 8, :]
                    rp = jnp.where(lane8 == 127, 0.0, pltpu.roll(mid, 127, 1))
                    rm = jnp.where(lane8 == 0, 0.0, pltpu.roll(mid, 1, 1))
                    deltas[0, p, ti] = ap - am
                    deltas[1, p, ti] = tp - tm
                    deltas[2, p, ti] = rp - rm
                    total = (ap + am) + (tp + tm) + (rp + rm)
                    add((p, w, ti), DISSIPATION * total - 6 * DISSIPATION * mid)
                    turn = frequency * mid
                    add((1 - p, w, ti), turn if p == 1 else -turn)
            for d in range(3):
                for c in range(VARS):
                    jac = jb[(d * VARS + w) * VARS + c, l - 1]
                    for ti in range(2):
                        for p in range(2):
                            add((p, c, ti), jac * deltas[d, p, ti])
        for ti, base in enumerate(bases):
            here = dt[l - 1, base : base + 8, :] * weight
            for p in range(2):
                for c in range(VARS):
                    forced = (
                        forcing(p, c, l, base)
                        + acc[p, c, ti]
                    )
                    value = v[0, p, c, l, base : base + 8, :] + here * forced
                    if q == SECTIONS - 1:
                        out[0, p, c, l - 1, base - PAD : base - PAD + 8, :] = value
                    else:
                        v[q + 1, p, c, l, base : base + 8, :] = value

    middle, sides = (PAD + 8, PAD + 16), (PAD, PAD + 24)

    def stencil(q, first, last, *pairs):
        def layer(l, carry):
            for pair in pairs or (middle, sides):
                tile_pair(q, l, pair)
            return carry

        lax.fori_loop(first, last, layer, 0)

    def outer_layers(q):
        def layer(i, carry):
            for pair in (middle, sides):
                tile_pair(q, 1 + (LAYERS - 1) * i, pair)
            return carry

        lax.fori_loop(jnp.where(inlet, 1, 0), jnp.where(outlet, 1, 2), layer, 0)

    def forward(q):
        blocks = []
        for c in range(VARS):
            blocks.append(
                jnp.concatenate(
                    [v[q, p, c, edge, PAD : PAD + SECTOR, :] for p in range(2)], axis=0
                )
            )
        x = jnp.concatenate(blocks, axis=1)
        hi = x.astype(BF16)
        lo = (x - hi.astype(F32)).astype(BF16)
        rhs = jnp.concatenate([hi, lo, hi, jnp.zeros_like(hi)], axis=0)
        res = jnp.dot(wf[...], rhs, preferred_element_type=F32)
        for c in range(VARS):
            parts[pl.ds(32 * c, 32), :] = res[:, 128 * c : 128 * (c + 1)]

    def pack_rows(q, at_):
        total = jnp.zeros((32, 128), F32)
        for i in range(4):
            rows = spare[pl.ds(i, 32, stride=4), :]
            shift = (32 * i - at_) % 128
            rows = pltpu.roll(rows, shift, 1) if shift else rows
            total = jnp.where(lanes(32) // 32 == i, rows, total)
        for b in range(nth):
            sent_x[q, b] = total[2 * b : 2 * b + 2]

    def stage_parts(q):
        sent[q] = parts[pl.ds(0, 128), :].T.reshape(nth, BAND, 128)
        spare[...] = parts[pl.ds(128, 128), :].T
        pack_rows(q, 0)
        if q == 0:
            pack_rows(SECTIONS, 32)

    def send_parts(q):
        def one(i, carry):
            band = far_first(i)
            mine = on_my_side(band)
            own = jnp.logical_and(mine, band == t)
            slot = jnp.where(mine, t, nth + t)
            which = jnp.where(mine, 0, 1)
            ways = [
                (sent.at[q, band], got.at[q, slot], p_send.at[q], p_recv.at[q, which]),
                (sent_x.at[q, band], got_x.at[q, slot], x_send.at[q], x_recv.at[q, which]),
            ]
            if q == 0:
                ways.append(
                    (
                        sent_x.at[SECTIONS, band], got_dt.at[slot],
                        x_send.at[SECTIONS], x_recv.at[SECTIONS, which],
                    )
                )

            @pl.when(own)
            def _():
                for here, there, _, recv in ways:
                    pltpu.make_async_copy(here, there, recv).start()

            @pl.when(jnp.logical_not(own))
            def _():
                device = (jnp.where(mine, y, py), band, jnp.where(mine, a, pa))
                for here, there, send, recv in ways:
                    remote(here, there, send, recv, device).start()

            return carry

        lax.fori_loop(0, nth, one, 0, unroll=4)

    def swapped(x):
        return jnp.where(lane8 < MODES, pltpu.roll(x, 128 - MODES, 1), pltpu.roll(x, MODES, 1))

    def mixed(slot, coeffs, neighbour):
        turned = [swapped(x) for x in coeffs]
        turned_n = [swapped(x) for x in neighbour]
        result = []
        for c in range(VARS):
            total = jnp.zeros((8, 128), F32)
            for w in range(VARS):
                i = c * VARS + w
                total = total + pack[slot, pl.ds(i, 1), :] * coeffs[w]
                total = total + pack[slot, pl.ds(25 + i, 1), :] * turned[w]
                total = total + pack[slot, pl.ds(50 + i, 1), :] * neighbour[w]
                total = total + pack[slot, pl.ds(75 + i, 1), :] * turned_n[w]
            result.append(jnp.where(lane8 < 2 * MODES, total, 0.0))
        return result

    def response(slot, coeffs):
        blocks = []
        for x in coeffs:
            hi = high(x)
            blocks.append(hi + pltpu.roll(hi, 32, 1) + pltpu.roll(x - hi, 64, 1))
        lhs = jnp.concatenate(blocks + [blocks[0]], axis=0).astype(BF16)
        fix = jnp.dot(lhs, e_tab[slot], preferred_element_type=F32)
        cells = dt_all[slot]
        cells = jnp.concatenate([cells, cells], axis=1)
        fix = fix * jnp.concatenate([cells] * (VARS + 1), axis=0)
        hi = fix.astype(BF16)
        lo = (fix - hi.astype(F32)).astype(BF16)
        res = lax.dot_general(
            jnp.concatenate([hi, lo], axis=0),
            e_tab[slot],
            (((1,), (1,)), ((), ())),
            preferred_element_type=F32,
        )
        half = BAND * (VARS + 1)
        result = []
        for c in range(VARS):
            top = res[BAND * c : BAND * (c + 1)]
            low = res[half + BAND * c : half + BAND * (c + 1)]
            result.append(top + pltpu.roll(top, 96, 1) + low)
        return result

    sub8 = subs(8)

    def unpacked(rows, at_=0):
        wide = jnp.where(sub8 < 4, rows[0:1], rows[1:2])
        result = wide
        for i in range(4):
            shift = (at_ - 32 * i) % 128
            turned = pltpu.roll(wide, shift, 1) if shift else wide
            result = jnp.where(lax.rem(sub8, 4) == i, turned, result)
        return result

    def packed(x):
        total = jnp.zeros((8, 128), F32)
        for i in range(4):
            turned = pltpu.roll(x, 32 * i, 1) if i else x
            total = jnp.where(lax.rem(sub8, 4) == i, turned, total)
        return jnp.concatenate(
            [
                jnp.sum(total[0:4], axis=0, keepdims=True),
                jnp.sum(total[4:8], axis=0, keepdims=True),
            ],
            axis=0,
        )

    def sums(q):
        def arrive(which):
            wait_for(got.at[q, pl.ds(which * nth, nth)], p_recv.at[q, which])
            wait_for(got_x.at[q, pl.ds(which * nth, nth)], x_recv.at[q, which])
            if q == 0:
                wait_for(
                    got_dt.at[pl.ds(which * nth, nth)], x_recv.at[SECTIONS, which]
                )

        arrive(0)
        pl.when(paired)(lambda: arrive(1))
        result = []
        for slot in range(2):
            total, last = got[q, slot * nth], got_x[q, slot * nth]
            for i in range(1, nth):
                total = total + got[q, slot * nth + i]
                last = last + got_x[q, slot * nth + i]
            pieces = [pltpu.roll(total, 128 - 32 * g, 1) if g else total for g in range(4)]
            pieces.append(unpacked(last))
            if slot == 1:
                pieces = [jnp.where(paired, x, 0.0) for x in pieces]
            result.append(pieces)
        return result

    def gather_steps():
        for slot in range(2):
            for u in range(nth // 4):
                cells = jnp.zeros((8, 128), F32)
                for i in range(4):
                    tile = unpacked(got_dt[slot * nth + 4 * u + i], 32 * i)
                    cells = jnp.where(lane8 // 32 == i, tile, cells)
                dt_all[slot, :, 128 * u : 128 * (u + 1)] = cells

    def send_modes(q, own, neighbour):
        for slot, values in ((0, own), (1, neighbour)):
            total = values[0]
            for i in range(1, 4):
                total = total + pltpu.roll(values[i], 32 * i, 1)
            c_out[q, slot] = total
            c_out_x[q, slot] = packed(values[4])

        def one(i, carry):
            theta = far_first(i)

            def send(slot, device):
                remote(
                    c_out.at[q, slot], c_in.at[q, t], c_send.at[q], c_recv.at[q], device
                ).start()
                remote(
                    c_out_x.at[q, slot], c_in_x.at[q, t], y_send.at[q], y_recv.at[q], device
                ).start()

            pl.when(paired)(lambda: send(1, (py, theta, pa)))
            pl.when(theta != t)(lambda: send(0, (y, theta, a)))

            @pl.when(theta == t)
            def _():
                pltpu.make_async_copy(
                    c_out.at[q, 0], c_in.at[q, t], c_recv.at[q]
                ).start()
                pltpu.make_async_copy(
                    c_out_x.at[q, 0], c_in_x.at[q, t], y_recv.at[q]
                ).start()

            return carry

        lax.fori_loop(0, nth, one, 0, unroll=4)

    def serve(q):
        own, nbr = sums(q)
        c_own = mixed(0, own, nbr)
        c_nbr = mixed(1, nbr, own)
        send_modes(q, c_own, c_nbr)
        if q == 0:
            gather_steps()
        scale = 1.0 / (SECTIONS - q) / circle
        r_own, r_nbr = response(0, c_own), response(1, c_nbr)
        own, nbr = sums(q + 1)
        own = [x - scale * r for x, r in zip(own, r_own)]
        nbr = [jnp.where(paired, x - scale * r, 0.0) for x, r in zip(nbr, r_nbr)]
        send_modes(q + 1, mixed(0, own, nbr), mixed(1, nbr, own))

    def fix_of(q):
        wait_for(c_in.at[q], c_recv.at[q])
        wait_for(c_in_x.at[q], y_recv.at[q])
        block = c_in[q].reshape(RADII, 128).T
        rows = [block[32 * i : 32 * (i + 1)] for i in range(4)]
        for b in range(nth):
            parts[pl.ds(2 * b, 2), :] = c_in_x[q, b]
        last = parts[pl.ds(0, 32), :]
        for i in range(4):
            spare[pl.ds(i, 32, stride=4), :] = (
                pltpu.roll(last, 128 - 32 * i, 1) if i else last
            )
        rows.append(spare[...].T[0:32])
        x = jnp.concatenate(rows, axis=1)
        hi = x.astype(BF16)
        lo = (x - hi.astype(F32)).astype(BF16)
        rhs = jnp.concatenate([hi, lo, hi, jnp.zeros_like(hi)], axis=0)
        return jnp.dot(w2[...], rhs, preferred_element_type=F32)

    def subtract(q, fix, margin):
        weight = 1.0 / (SECTIONS - q)
        rows = SECTOR + 2 * margin
        base = PAD - margin
        here = dt[edge - 1, base : base + rows, :] * weight
        for p in range(2):
            for c in range(VARS):
                top = 48 * p + 8 - margin
                less = here * fix[top : top + rows, 128 * c : 128 * (c + 1)]
                if q == SECTIONS - 1:
                    out[0, p, c, edge - 1] = out[0, p, c, edge - 1] - less
                else:
                    v[q + 1, p, c, edge, base : base + rows, :] = (
                        v[q + 1, p, c, edge, base : base + rows, :] - less
                    )

    def edge_copies():
        plane = edge - 1
        copies = []
        for i, (at_, row, device) in enumerate(
            ((0, PAD + SECTOR, t_prev), (SECTOR - 8, PAD - 8, t_next))
        ):
            rows, place, device = pl.ds(at_, 8), pl.ds(row, 8), (y, device, a)
            copies += [
                remote(
                    v.at[0, :, :, edge, pl.ds(PAD + at_, 8)], v.at[0, :, :, edge, place],
                    edge_send.at[0, i], edge_recv.at[0, i], device,
                ),
                remote(
                    step_in.at[0, plane, rows], dt.at[plane, place],
                    edge_send.at[1, i], edge_recv.at[1, i], device,
                ),
                remote(
                    source_in.at[0, :, :, plane, rows], src_edge.at[1 - i],
                    edge_send.at[2, i], edge_recv.at[2, i], device,
                ),
            ]
        return copies

    def plane_tile(i):
        return v.at[0, :, :, edge, pl.ds((PAD + SECTOR, PAD - 8)[i], 8)]

    def tile_copies():
        return [
            remote(
                v.at[1, :, :, edge, pl.ds(at_, 8)], v.at[1, :, :, edge, pl.ds(row, 8)],
                tile_send.at[i], tile_recv.at[i], (y, device, a),
            )
            for i, (at_, row, device) in enumerate(
                ((PAD, PAD + SECTOR, t_prev), (PAD + SECTOR - 8, PAD - 8, t_next))
            )
        ]

    def pack_copy():
        return remote(pack.at[0], pack.at[1], pk_sem.at[0], pk_sem.at[1], (py, t, pa))

    helps = jnp.logical_and(bnd, jnp.logical_not(owner))
    served = jnp.logical_and(owner, paired)

    load_jac.wait()

    def spread(l, carry):
        for d in range(3):
            for w in range(VARS):
                for c in range(VARS):
                    jb[(d * VARS + w) * VARS + c, l] = jnp.broadcast_to(
                        jin[d, w, c, pl.ds(l, 1), :] * 0.5, (8, 128)
                    )
        return carry

    lax.fori_loop(0, LAYERS, spread, 0)
    load_state.wait()
    load_step.wait()

    @pl.when(bnd)
    def _():
        parts[pl.ds(160, 32), :] = dt[edge - 1, PAD : PAD + SECTOR, :]
        forward(0)
        stage_parts(0)

    stage_theta(0)

    pl.semaphore_wait(
        barrier,
        2
        + jnp.where(a > 0, 1, 0)
        + jnp.where(a < nax - 1, 1, 0)
        + jnp.where(
            bnd,
            jnp.where(owner, jnp.where(paired, 2 * nth - 1, nth - 1), nth),
            0,
        ),
    )


    @pl.when(bnd)
    def _():
        copies = edge_copies()
        for copy in copies[::3]:
            copy.start()
        send_parts(0)
        for i in (1, 4, 2, 5):
            copies[i].start()
        pl.when(helps)(lambda: pack_copy().start())

    for copy in theta_copies(0):
        copy.start()
    send_axial(0)
    load_source.wait()

    far = (jnp.where(inlet, 3, 2), jnp.where(outlet, LAYERS - 1, LAYERS))
    near = jnp.where(inlet, 1, LAYERS - 1)
    second = jnp.where(inlet, 2, LAYERS - 1)

    for q in (0, 2):

        @pl.when(bnd)
        def _():
            if q == 0:
                for i in range(2):
                    wait_for(plane_tile(i), edge_recv.at[0, i])
            else:
                forward(q)
                stage_parts(q)
                send_parts(q)
            for pair in (middle, sides):
                tile_pair(q, edge, pair)
            forward(q + 1)
            stage_parts(q + 1)
            send_parts(q + 1)
            if q == 0:
                for copy in tile_copies():
                    copy.start()

        if q:
            send_theta(q)
        stencil(q, 2, LAYERS, middle)
        take_theta(q)
        stencil(q, 2, LAYERS, sides)
        if q == 0:

            @pl.when(served)
            def _():
                pack_copy().wait_recv()
                full_table(1)

        take_axial(q)
        outer_layers(q)
        send_theta(q + 1)
        send_axial(q + 1)
        pl.when(owner)(lambda: serve(q))
        stencil(q + 1, *far, middle)
        if q == 0:

            @pl.when(bnd)
            def _():
                for copy in tile_copies():
                    copy.wait()

        take_theta(q + 1)
        stencil(q + 1, *far, sides)
        take_axial(q + 1)
        outer_layers(q + 1)
        if q == 0:
            send_axial(q + 2)

        @pl.when(bnd)
        def _():
            now = fix_of(q)
            if q == 0:
                for i in range(2):
                    wait_for(dt.at[edge - 1, pl.ds(PAD, 8)], edge_recv.at[1, i])
                    wait_for(src_edge.at[i], edge_recv.at[2, i])
                subtract(q, now, 8)
                for third in range(3):
                    first = PAD - 8 + 16 * third
                    tile_pair(q + 1, edge, (first, first + 8))
                stencil(q + 1, second, second + 1)
                subtract(q + 1, fix_of(q + 1), 8)
            else:
                subtract(q, now, 8)
                stencil(q + 1, near, near + 2)
                subtract(q + 1, fix_of(q + 1), 0)

    for q in range(SECTIONS):
        for copy in theta_copies(q):
            copy.wait_send()
        pl.when(a > 0)(lambda: axial_down(q).wait_send())
        pl.when(a < nax - 1)(lambda: axial_up(q).wait_send())

    @pl.when(bnd)
    def _():
        for copy in edge_copies():
            copy.wait_send()
        pl.when(helps)(lambda: pack_copy().wait_send())
        for q in range(SECTIONS):
            alike = ((sent, p_send, got, c_send), (sent_x, x_send, got_x, y_send))
            for mine, mine_sem, theirs, theirs_sem in alike:
                pl.when(owner)(
                    lambda: wait_for(mine.at[q, pl.ds(0, nth - 1)], mine_sem.at[q])
                )
                pl.when(helps)(lambda: wait_for(mine.at[q], mine_sem.at[q]))
                pl.when(served)(
                    lambda: wait_for(theirs.at[q, pl.ds(0, 2 * nth - 1)], theirs_sem.at[q])
                )
                pl.when(jnp.logical_and(owner, alone))(
                    lambda: wait_for(theirs.at[q, pl.ds(0, nth - 1)], theirs_sem.at[q])
                )
        pl.when(owner)(
            lambda: wait_for(
                sent_x.at[SECTIONS, pl.ds(0, nth - 1)], x_send.at[SECTIONS]
            )
        )
        pl.when(helps)(lambda: wait_for(sent_x.at[SECTIONS], x_send.at[SECTIONS]))


def solution(mesh):
    nrow, nth, nax = mesh.shape["row"], mesh.shape["theta"], mesh.shape["axial"]

    def step(state, source, time_step, jacobian, blade, order, giles, coupling):
        circle = order.shape[1]
        giles = giles.transpose(0, 1, 2, 4, 3, 5)
        coupling = coupling.transpose(0, 1, 3, 2, 4)
        cells = (2, VARS)
        anyspace = pl.BlockSpec(memory_space=pl.ANY)
        scalars = pl.BlockSpec(memory_space=pltpu.SMEM)
        dma = pltpu.SemaphoreType.DMA
        return pl.pallas_call(
            functools.partial(kernel, (nrow, nth, nax, circle)),
            out_shape=pltpu.VMEM(state.shape, F32),
            in_specs=[anyspace] * 7 + [scalars],
            out_specs=pl.BlockSpec(memory_space=pltpu.VMEM),
            scratch_shapes=[
                pltpu.SMEM(order.shape, jnp.int32),
                pltpu.SMEM(giles.shape, F32),
                pltpu.SMEM(coupling.shape, F32),
                pltpu.VMEM((SECTIONS, *cells, LAYERS + 2, 2 * PAD + SECTOR, RADII), F32),
                pltpu.VMEM((*cells, LAYERS, SECTOR, RADII), F32),
                pltpu.VMEM((2, *cells, 8, RADII), F32),
                pltpu.VMEM((LAYERS, 2 * PAD + SECTOR, RADII), F32),
                pltpu.VMEM((3, VARS, VARS, LAYERS, RADII), F32),
                pltpu.VMEM((75, LAYERS, 8, RADII), F32),
                pltpu.VMEM((SECTIONS, 2, *cells, LAYERS, RADII), F32),
                pltpu.VMEM((SECTIONS, 2, *cells, LAYERS, RADII), F32),
                pltpu.VMEM((32, 256), BF16),
                pltpu.VMEM((2 * (SECTOR + 16), 128), BF16),
                pltpu.VMEM((2, 128, 2 * circle), BF16),
                pltpu.VMEM((2, 104, 128), F32),
                pltpu.VMEM((256, 128), F32),
                pltpu.VMEM((SECTIONS, nth, BAND, 128), F32),
                pltpu.VMEM((SECTIONS + 1, nth, 2, 128), F32),
                pltpu.VMEM((SECTIONS, 2 * nth, BAND, 128), F32),
                pltpu.VMEM((SECTIONS, 2 * nth, 2, 128), F32),
                pltpu.VMEM((2 * nth, 2, 128), F32),
                pltpu.VMEM((2, BAND, circle), F32),
                pltpu.VMEM((SECTIONS, 2, BAND, 128), F32),
                pltpu.VMEM((SECTIONS, 2, 2, 128), F32),
                pltpu.VMEM((SECTIONS, nth, BAND, 128), F32),
                pltpu.VMEM((SECTIONS, nth, 2, 128), F32),
                pltpu.VMEM((RADII, 128), F32),
                dma((7,)),
                dma((SECTIONS, 2)),
                dma((SECTIONS, 2)),
                dma((SECTIONS, 2)),
                dma((SECTIONS, 2)),
                dma((3, 2)),
                dma((3, 2)),
                dma((2,)),
                dma((2,)),
                dma((2,)),
                dma((SECTIONS,)),
                dma((SECTIONS, 2)),
                dma((SECTIONS + 1,)),
                dma((SECTIONS + 1, 2)),
                dma((SECTIONS,)),
                dma((SECTIONS,)),
                dma((SECTIONS,)),
                dma((SECTIONS,)),
            ],
            compiler_params=pltpu.CompilerParams(
                collective_id=0, has_side_effects=True, vmem_limit_bytes=VMEM_LIMIT
            ),
        )(
            *(
                pltpu.with_memory_space_constraint(x, pltpu.HBM)
                for x in (state, source, time_step, jacobian, order, giles, coupling)
            ),
            blade,
        )

    return jax.shard_map(
        step,
        mesh=mesh,
        in_specs=(
            P("row", None, None, "axial", "theta", None),
            P("row", None, None, "axial", "theta", None),
            P("row", "axial", "theta", None),
            P("row", None, None, None, "axial", None),
            P("row"),
            P("row", None),
            P("row", None, None, None, None, None),
            P("row", None, None, None, None),
        ),
        out_specs=P("row", None, None, "axial", "theta", None),
        check_vma=False,
    )
```

```python
import functools
import math

import jax
import jax.numpy as jnp
from jax import lax
from jax.experimental import pallas as pl
from jax.experimental.pallas import tpu as pltpu
from jax.sharding import PartitionSpec as P

MESH = pl.DeviceIdType.MESH
F32 = jnp.float32
BF16 = jnp.bfloat16
MODES = 16
SECTIONS = 4
DISSIPATION = 0.05
OMEGA_UNIT = 0.02
LAYERS = 8
SECTOR = 32
RADII = 128
VARS = 5
PAD = 16
FIRST, LAST = PAD, PAD + SECTOR - 1
OWN = pl.ds(PAD, SECTOR)
BAND = 8
MODE_ROW = 100
VMEM_LIMIT = 48 * 2**20


def sin_cos(turns):
    h = (turns - jnp.floor(turns + 0.5)) * math.pi
    z = h * h
    s = 1.0 / 6227020800
    for d in (-39916800, 362880, -5040, 120, -6, 1):
        s = s * z + 1.0 / d
    s = s * h
    c = 1.0 / 479001600
    for d in (-3628800, 40320, -720, 24, -2, 1):
        c = c * z + 1.0 / d
    return 2.0 * s * c, 1.0 - 2.0 * s * s


def high(x):
    return x.astype(BF16).astype(F32)


def lanes(rows):
    return lax.broadcasted_iota(jnp.int32, (rows, 128), 1)


def subs(rows):
    return lax.broadcasted_iota(jnp.int32, (rows, 128), 0)


def wait_for(ref, sem):
    pltpu.make_async_copy(ref, ref, sem).wait()


def kernel(
    shape,
    state_in,
    source_in,
    step_in,
    jac_in,
    order_in,
    giles_in,
    coupling_in,
    blade,
    out,
    order,
    giles,
    coupling,
    v,
    src,
    src_edge,
    dt,
    jin,
    jb,
    t_out,
    t_in,
    wf,
    w2,
    e_tab,
    pack,
    parts,
    sent,
    sent_x,
    got,
    got_x,
    got_dt,
    dt_all,
    c_out,
    c_out_x,
    c_in,
    c_in_x,
    spare,
    load_sem,
    th_send,
    th_recv,
    ax_send,
    ax_recv,
    edge_send,
    edge_recv,
    tile_send,
    tile_recv,
    pk_sem,
    p_send,
    p_recv,
    x_send,
    x_recv,
    c_send,
    c_recv,
    y_send,
    y_recv,
):
    nrow, nth, nax, circle = shape
    y, t, a = lax.axis_index("row"), lax.axis_index("theta"), lax.axis_index("axial")
    inlet, outlet = a == 0, a == nax - 1
    bnd = jnp.logical_or(inlet, outlet)
    side = jnp.where(inlet, 0, 1)
    paired = jnp.logical_or(
        jnp.logical_and(inlet, y > 0), jnp.logical_and(outlet, y < nrow - 1)
    )
    alone = jnp.logical_not(paired)
    py = jnp.where(paired, jnp.where(inlet, y - 1, y + 1), y)
    pa = jnp.where(paired, jnp.where(inlet, nax - 1, 0), a)
    edge = jnp.where(inlet, 1, LAYERS)

    def on_my_side(band):
        return jnp.logical_or(alone, lax.rem(band // 2, 2) == side)

    owner = jnp.logical_and(bnd, on_my_side(t))
    nz = nth // 2

    def far_first(i):
        step = i // 2
        away = (step + 1) // 2
        dz = nz // 2 + jnp.where(lax.rem(step, 2) == 0, away, -away)
        return 2 * lax.rem(t // 2 + dz, nz) + lax.rem(i, 2)

    t_next, t_prev = lax.rem(t + 1, nth), lax.rem(t + nth - 1, nth)

    load_state = pltpu.make_async_copy(
        state_in.at[0], v.at[0, :, :, pl.ds(1, LAYERS), OWN], load_sem.at[0]
    )
    load_step = pltpu.make_async_copy(step_in.at[0], dt.at[:, OWN], load_sem.at[1])
    load_jac = pltpu.make_async_copy(jac_in.at[0], jin, load_sem.at[2])
    load_source = pltpu.make_async_copy(source_in.at[0], src, load_sem.at[3])
    load_small = [
        pltpu.make_async_copy(order_in, order, load_sem.at[4]),
        pltpu.make_async_copy(giles_in, giles, load_sem.at[5]),
        pltpu.make_async_copy(coupling_in, coupling, load_sem.at[6]),
    ]
    load_state.start()

    barrier = pltpu.get_barrier_semaphore()

    def hello(row, theta, axial):
        pl.semaphore_signal(
            barrier, inc=1, device_id=(row, theta, axial), device_id_type=MESH
        )

    hello(y, t_next, a)
    hello(y, t_prev, a)
    pl.when(a > 0)(lambda: hello(y, t, a - 1))
    pl.when(a < nax - 1)(lambda: hello(y, t, a + 1))

    @pl.when(bnd)
    def _():
        def greet(i, carry):
            other = far_first(i)
            mine = on_my_side(other)

            @pl.when(jnp.logical_and(other != t, jnp.logical_or(owner, mine)))
            def _():
                hello(y, other, a)

            @pl.when(
                jnp.logical_and(
                    paired, jnp.logical_or(owner, jnp.logical_not(mine))
                )
            )
            def _():
                hello(py, other, pa)

            return carry

        lax.fori_loop(0, nth, greet, 0)

    load_step.start()

    @pl.when(bnd)
    def _():
        for copy in load_small:
            copy.start()

    load_jac.start()
    load_source.start()

    lane1, lane16, sub16 = lanes(1), lanes(16), subs(16)

    def mode_column(slot):
        row = pack[slot, pl.ds(MODE_ROW, 1), :]
        picked = jnp.where(lane16 == sub16, jnp.broadcast_to(row, (16, 128)), 0.0)
        return jnp.sum(picked, axis=1, keepdims=True)

    def full_table(slot):
        column = mode_column(slot)
        wide = lax.broadcasted_iota(jnp.int32, (16, circle), 1).astype(F32)
        sn, cs = sin_cos(wide * column * (1.0 / circle))
        table = jnp.concatenate(
            [
                jnp.concatenate([cs, sn], axis=1),
                jnp.concatenate([-sn, cs], axis=1),
            ],
            axis=0,
        )
        hi = table.astype(BF16)
        lo = (table - hi.astype(F32)).astype(BF16)
        e_tab[slot] = jnp.concatenate([hi, lo, hi, jnp.zeros_like(hi)], axis=0)

    @pl.when(bnd)
    def _():
        for copy in load_small:
            copy.wait()
        mrow = jnp.zeros((1, 128), F32)
        for k in range(MODES):
            m_k = order[0, k].astype(F32) - (circle // 2)
            mrow = jnp.where(lax.rem(lane1, MODES) == k, m_k, mrow)
        pack[0, pl.ds(MODE_ROW, 1), :] = mrow
        slope = mrow * (2.0 / circle)
        sign = jnp.where(lax.rem(lane1, 2 * MODES) < MODES, -1.0, 1.0)
        for c in range(VARS):
            for w in range(VARS):
                i = c * VARS + w
                pack[0, pl.ds(i, 1), :] = (
                    giles[0, side, 0, c, 0, w] + slope * giles[0, side, 1, c, 0, w]
                )
                pack[0, pl.ds(25 + i, 1), :] = sign * (
                    giles[0, side, 0, c, 1, w] + slope * giles[0, side, 1, c, 1, w]
                )
                pack[0, pl.ds(50 + i, 1), :] = jnp.broadcast_to(
                    coupling[0, side, c, 0, w], (1, 128)
                )
                pack[0, pl.ds(75 + i, 1), :] = sign * coupling[0, side, c, 1, w]
        first_cell = (t * SECTOR).astype(F32)
        cell = first_cell + lax.rem(lane16, SECTOR).astype(F32)
        sn, cs = sin_cos(cell * mode_column(0) * (1.0 / circle))
        real = lax.rem(lane16, 2 * SECTOR) < SECTOR
        table = jnp.concatenate(
            [jnp.where(real, cs, sn), jnp.where(real, -sn, cs)], axis=0
        ) * (1.0 / circle)
        hi = high(table)
        lo = jnp.where(lanes(32) < 64, table - hi, 0.0)
        wf[...] = jnp.concatenate([hi, lo], axis=1).astype(BF16)
        rows = SECTOR + 16
        cell = first_cell - 8.0 + subs(rows).astype(F32)
        sn, cs = sin_cos(cell * mrow * (1.0 / circle))
        real = lax.rem(lanes(rows), 2 * MODES) < MODES
        table = jnp.concatenate(
            [jnp.where(real, cs, -sn), jnp.where(real, sn, cs)], axis=0
        )
        hi = high(table)
        lane = lanes(2 * rows)
        w2[...] = jnp.where(
            lane < 64, hi, jnp.where(lane < 96, table - hi, 0.0)
        ).astype(BF16)
        parts[pl.ds(160, 96), :] = jnp.zeros((96, 128), F32)

    pl.when(owner)(lambda: full_table(0))

    @pl.when(inlet)
    def _():
        for q in range(SECTIONS):
            v[q, :, :, 0, :, :] = jnp.zeros((2, VARS, 2 * PAD + SECTOR, 128), F32)

    @pl.when(outlet)
    def _():
        for q in range(SECTIONS):
            v[q, :, :, LAYERS + 1, :, :] = jnp.zeros(
                (2, VARS, 2 * PAD + SECTOR, 128), F32
            )

    def remote(src_ref, dst_ref, send, recv, device):
        return pltpu.make_async_remote_copy(
            src_ref=src_ref,
            dst_ref=dst_ref,
            send_sem=send,
            recv_sem=recv,
            device_id=device,
            device_id_type=MESH,
        )

    def theta_copies(q):
        return [
            remote(
                t_out.at[q, i], t_in.at[q, 1 - i], th_send.at[q, i],
                th_recv.at[q, 1 - i], (y, (t_prev, t_next)[i], a),
            )
            for i in range(2)
        ]

    def flat(q, p, c):
        return v.at[q, p, c].reshape((LAYERS + 2) * (2 * PAD + SECTOR), RADII)

    def column(row):
        return pl.ds(2 * PAD + SECTOR + row, LAYERS, stride=2 * PAD + SECTOR)

    def stage_theta(q):
        for p in range(2):
            for c in range(VARS):
                rows = flat(q, p, c)
                t_out[q, 0, p, c] = rows[column(FIRST), :]
                t_out[q, 1, p, c] = rows[column(LAST), :]

    def send_theta(q):
        stage_theta(q)
        for copy in theta_copies(q):
            copy.start()

    def take_theta(q):
        for copy in theta_copies(q):
            copy.wait_recv()

        for p in range(2):
            for c in range(VARS):
                rows = flat(q, p, c)
                rows[column(FIRST - 1), :] = t_in[q, 0, p, c]
                rows[column(LAST + 1), :] = t_in[q, 1, p, c]

    def axial_down(q):
        return remote(
            v.at[q, :, :, 1, OWN], v.at[q, :, :, LAYERS + 1, OWN],
            ax_send.at[q, 0], ax_recv.at[q, 1], (y, t, a - 1),
        )

    def axial_up(q):
        return remote(
            v.at[q, :, :, LAYERS, OWN], v.at[q, :, :, 0, OWN],
            ax_send.at[q, 1], ax_recv.at[q, 0], (y, t, a + 1),
        )

    def send_axial(q):
        pl.when(a > 0)(lambda: axial_down(q).start())
        pl.when(a < nax - 1)(lambda: axial_up(q).start())

    def take_axial(q):
        pl.when(a > 0)(lambda: wait_for(v.at[q, :, :, 0, OWN], ax_recv.at[q, 0]))
        pl.when(a < nax - 1)(
            lambda: wait_for(v.at[q, :, :, LAYERS + 1, OWN], ax_recv.at[q, 1])
        )

    frequency = blade[0].astype(F32) * OMEGA_UNIT
    lane8 = lanes(8)

    def forcing(p, c, l, base):
        if base < PAD:
            return src_edge[0, p, c]
        if base >= PAD + SECTOR:
            return src_edge[1, p, c]
        return src[p, c, l - 1, base - PAD : base - PAD + 8, :]

    def tile_pair(q, l, bases):
        weight = 1.0 / (SECTIONS - q)
        acc = {}

        def add(key, value):
            acc[key] = acc[key] + value if key in acc else value

        for w in range(VARS):
            deltas = {}
            for ti, base in enumerate(bases):
                for p in range(2):
                    mid = v[q, p, w, l, base : base + 8, :]
                    tp = v[q, p, w, l, base + 1 : base + 9, :]
                    tm = v[q, p, w, l, base - 1 : base + 7, :]
                    ap = v[q, p, w, l + 1, base : base + 8, :]
                    am = v[q, p, w, l - 1, base : base + 8, :]
                    rp = jnp.where(lane8 == 127, 0.0, pltpu.roll(mid, 127, 1))
                    rm = jnp.where(lane8 == 0, 0.0, pltpu.roll(mid, 1, 1))
                    deltas[0, p, ti] = ap - am
                    deltas[1, p, ti] = tp - tm
                    deltas[2, p, ti] = rp - rm
                    total = (ap + am) + (tp + tm) + (rp + rm)
                    add((p, w, ti), DISSIPATION * total - 6 * DISSIPATION * mid)
                    turn = frequency * mid
                    add((1 - p, w, ti), turn if p == 1 else -turn)
            for d in range(3):
                for c in range(VARS):
                    jac = jb[(d * VARS + w) * VARS + c, l - 1]
                    for ti in range(2):
                        for p in range(2):
                            add((p, c, ti), jac * deltas[d, p, ti])
        for ti, base in enumerate(bases):
            here = dt[l - 1, base : base + 8, :] * weight
            for p in range(2):
                for c in range(VARS):
                    forced = (
                        forcing(p, c, l, base)
                        + acc[p, c, ti]
                    )
                    value = v[0, p, c, l, base : base + 8, :] + here * forced
                    if q == SECTIONS - 1:
                        out[0, p, c, l - 1, base - PAD : base - PAD + 8, :] = value
                    else:
                        v[q + 1, p, c, l, base : base + 8, :] = value

    middle, sides = (PAD + 8, PAD + 16), (PAD, PAD + 24)

    def stencil(q, first, last, *pairs):
        def layer(l, carry):
            for pair in pairs or (middle, sides):
                tile_pair(q, l, pair)
            return carry

        lax.fori_loop(first, last, layer, 0)

    def outer_layers(q):
        def layer(i, carry):
            for pair in (middle, sides):
                tile_pair(q, 1 + (LAYERS - 1) * i, pair)
            return carry

        lax.fori_loop(jnp.where(inlet, 1, 0), jnp.where(outlet, 1, 2), layer, 0)

    def forward(q):
        blocks = []
        for c in range(VARS):
            blocks.append(
                jnp.concatenate(
                    [v[q, p, c, edge, PAD : PAD + SECTOR, :] for p in range(2)], axis=0
                )
            )
        x = jnp.concatenate(blocks, axis=1)
        hi = x.astype(BF16)
        lo = (x - hi.astype(F32)).astype(BF16)
        rhs = jnp.concatenate([hi, lo, hi, jnp.zeros_like(hi)], axis=0)
        res = jnp.dot(wf[...], rhs, preferred_element_type=F32)
        for c in range(VARS):
            parts[pl.ds(32 * c, 32), :] = res[:, 128 * c : 128 * (c + 1)]

    def pack_rows(q, at_):
        total = jnp.zeros((32, 128), F32)
        for i in range(4):
            rows = spare[pl.ds(i, 32, stride=4), :]
            shift = (32 * i - at_) % 128
            rows = pltpu.roll(rows, shift, 1) if shift else rows
            total = jnp.where(lanes(32) // 32 == i, rows, total)
        for b in range(nth):
            sent_x[q, b] = total[2 * b : 2 * b + 2]

    def stage_parts(q):
        sent[q] = parts[pl.ds(0, 128), :].T.reshape(nth, BAND, 128)
        spare[...] = parts[pl.ds(128, 128), :].T
        pack_rows(q, 0)
        if q == 0:
            pack_rows(SECTIONS, 32)

    def send_parts(q):
        def one(i, carry):
            band = far_first(i)
            mine = on_my_side(band)
            own = jnp.logical_and(mine, band == t)
            slot = jnp.where(mine, t, nth + t)
            which = jnp.where(mine, 0, 1)
            ways = [
                (sent.at[q, band], got.at[q, slot], p_send.at[q], p_recv.at[q, which]),
                (sent_x.at[q, band], got_x.at[q, slot], x_send.at[q], x_recv.at[q, which]),
            ]
            if q == 0:
                ways.append(
                    (
                        sent_x.at[SECTIONS, band], got_dt.at[slot],
                        x_send.at[SECTIONS], x_recv.at[SECTIONS, which],
                    )
                )

            @pl.when(own)
            def _():
                for here, there, _, recv in ways:
                    pltpu.make_async_copy(here, there, recv).start()

            @pl.when(jnp.logical_not(own))
            def _():
                device = (jnp.where(mine, y, py), band, jnp.where(mine, a, pa))
                for here, there, send, recv in ways:
                    remote(here, there, send, recv, device).start()

            return carry

        lax.fori_loop(0, nth, one, 0, unroll=4)

    def swapped(x):
        return jnp.where(lane8 < MODES, pltpu.roll(x, 128 - MODES, 1), pltpu.roll(x, MODES, 1))

    def mixed(slot, coeffs, neighbour):
        turned = [swapped(x) for x in coeffs]
        turned_n = [swapped(x) for x in neighbour]
        result = []
        for c in range(VARS):
            total = jnp.zeros((8, 128), F32)
            for w in range(VARS):
                i = c * VARS + w
                total = total + pack[slot, pl.ds(i, 1), :] * coeffs[w]
                total = total + pack[slot, pl.ds(25 + i, 1), :] * turned[w]
                total = total + pack[slot, pl.ds(50 + i, 1), :] * neighbour[w]
                total = total + pack[slot, pl.ds(75 + i, 1), :] * turned_n[w]
            result.append(jnp.where(lane8 < 2 * MODES, total, 0.0))
        return result

    def response(slot, coeffs):
        blocks = []
        for x in coeffs:
            hi = high(x)
            blocks.append(hi + pltpu.roll(hi, 32, 1) + pltpu.roll(x - hi, 64, 1))
        lhs = jnp.concatenate(blocks + [blocks[0]], axis=0).astype(BF16)
        fix = jnp.dot(lhs, e_tab[slot], preferred_element_type=F32)
        cells = dt_all[slot]
        cells = jnp.concatenate([cells, cells], axis=1)
        fix = fix * jnp.concatenate([cells] * (VARS + 1), axis=0)
        hi = fix.astype(BF16)
        lo = (fix - hi.astype(F32)).astype(BF16)
        res = lax.dot_general(
            jnp.concatenate([hi, lo], axis=0),
            e_tab[slot],
            (((1,), (1,)), ((), ())),
            preferred_element_type=F32,
        )
        half = BAND * (VARS + 1)
        result = []
        for c in range(VARS):
            top = res[BAND * c : BAND * (c + 1)]
            low = res[half + BAND * c : half + BAND * (c + 1)]
            result.append(top + pltpu.roll(top, 96, 1) + low)
        return result

    sub8 = subs(8)

    def unpacked(rows, at_=0):
        wide = jnp.where(sub8 < 4, rows[0:1], rows[1:2])
        result = wide
        for i in range(4):
            shift = (at_ - 32 * i) % 128
            turned = pltpu.roll(wide, shift, 1) if shift else wide
            result = jnp.where(lax.rem(sub8, 4) == i, turned, result)
        return result

    def packed(x):
        total = jnp.zeros((8, 128), F32)
        for i in range(4):
            turned = pltpu.roll(x, 32 * i, 1) if i else x
            total = jnp.where(lax.rem(sub8, 4) == i, turned, total)
        return jnp.concatenate(
            [
                jnp.sum(total[0:4], axis=0, keepdims=True),
                jnp.sum(total[4:8], axis=0, keepdims=True),
            ],
            axis=0,
        )

    def sums(q):
        def arrive(which):
            wait_for(got.at[q, pl.ds(which * nth, nth)], p_recv.at[q, which])
            wait_for(got_x.at[q, pl.ds(which * nth, nth)], x_recv.at[q, which])
            if q == 0:
                wait_for(
                    got_dt.at[pl.ds(which * nth, nth)], x_recv.at[SECTIONS, which]
                )

        arrive(0)
        pl.when(paired)(lambda: arrive(1))
        result = []
        for slot in range(2):
            total, last = got[q, slot * nth], got_x[q, slot * nth]
            for i in range(1, nth):
                total = total + got[q, slot * nth + i]
                last = last + got_x[q, slot * nth + i]
            pieces = [pltpu.roll(total, 128 - 32 * g, 1) if g else total for g in range(4)]
            pieces.append(unpacked(last))
            if slot == 1:
                pieces = [jnp.where(paired, x, 0.0) for x in pieces]
            result.append(pieces)
        return result

    def gather_steps():
        for slot in range(2):
            for u in range(nth // 4):
                cells = jnp.zeros((8, 128), F32)
                for i in range(4):
                    tile = unpacked(got_dt[slot * nth + 4 * u + i], 32 * i)
                    cells = jnp.where(lane8 // 32 == i, tile, cells)
                dt_all[slot, :, 128 * u : 128 * (u + 1)] = cells

    def send_modes(q, own, neighbour):
        for slot, values in ((0, own), (1, neighbour)):
            total = values[0]
            for i in range(1, 4):
                total = total + pltpu.roll(values[i], 32 * i, 1)
            c_out[q, slot] = total
            c_out_x[q, slot] = packed(values[4])

        def one(i, carry):
            theta = far_first(i)

            def send(slot, device):
                remote(
                    c_out.at[q, slot], c_in.at[q, t], c_send.at[q], c_recv.at[q], device
                ).start()
                remote(
                    c_out_x.at[q, slot], c_in_x.at[q, t], y_send.at[q], y_recv.at[q], device
                ).start()

            pl.when(paired)(lambda: send(1, (py, theta, pa)))
            pl.when(theta != t)(lambda: send(0, (y, theta, a)))

            @pl.when(theta == t)
            def _():
                pltpu.make_async_copy(
                    c_out.at[q, 0], c_in.at[q, t], c_recv.at[q]
                ).start()
                pltpu.make_async_copy(
                    c_out_x.at[q, 0], c_in_x.at[q, t], y_recv.at[q]
                ).start()

            return carry

        lax.fori_loop(0, nth, one, 0, unroll=4)

    def serve(q):
        own, nbr = sums(q)
        c_own = mixed(0, own, nbr)
        c_nbr = mixed(1, nbr, own)
        send_modes(q, c_own, c_nbr)
        if q == 0:
            gather_steps()
        scale = 1.0 / (SECTIONS - q) / circle
        r_own, r_nbr = response(0, c_own), response(1, c_nbr)
        own, nbr = sums(q + 1)
        own = [x - scale * r for x, r in zip(own, r_own)]
        nbr = [jnp.where(paired, x - scale * r, 0.0) for x, r in zip(nbr, r_nbr)]
        send_modes(q + 1, mixed(0, own, nbr), mixed(1, nbr, own))

    def fix_of(q):
        wait_for(c_in.at[q], c_recv.at[q])
        wait_for(c_in_x.at[q], y_recv.at[q])
        block = c_in[q].reshape(RADII, 128).T
        rows = [block[32 * i : 32 * (i + 1)] for i in range(4)]
        for b in range(nth):
            parts[pl.ds(2 * b, 2), :] = c_in_x[q, b]
        last = parts[pl.ds(0, 32), :]
        for i in range(4):
            spare[pl.ds(i, 32, stride=4), :] = (
                pltpu.roll(last, 128 - 32 * i, 1) if i else last
            )
        rows.append(spare[...].T[0:32])
        x = jnp.concatenate(rows, axis=1)
        hi = x.astype(BF16)
        lo = (x - hi.astype(F32)).astype(BF16)
        rhs = jnp.concatenate([hi, lo, hi, jnp.zeros_like(hi)], axis=0)
        return jnp.dot(w2[...], rhs, preferred_element_type=F32)

    def subtract(q, fix, margin):
        weight = 1.0 / (SECTIONS - q)
        rows = SECTOR + 2 * margin
        base = PAD - margin
        here = dt[edge - 1, base : base + rows, :] * weight
        for p in range(2):
            for c in range(VARS):
                top = 48 * p + 8 - margin
                less = here * fix[top : top + rows, 128 * c : 128 * (c + 1)]
                if q == SECTIONS - 1:
                    out[0, p, c, edge - 1] = out[0, p, c, edge - 1] - less
                else:
                    v[q + 1, p, c, edge, base : base + rows, :] = (
                        v[q + 1, p, c, edge, base : base + rows, :] - less
                    )

    def edge_copies():
        plane = edge - 1
        copies = []
        for i, (at_, row, device) in enumerate(
            ((0, PAD + SECTOR, t_prev), (SECTOR - 8, PAD - 8, t_next))
        ):
            rows, place, device = pl.ds(at_, 8), pl.ds(row, 8), (y, device, a)
            copies += [
                remote(
                    v.at[0, :, :, edge, pl.ds(PAD + at_, 8)], v.at[0, :, :, edge, place],
                    edge_send.at[0, i], edge_recv.at[0, i], device,
                ),
                remote(
                    step_in.at[0, plane, rows], dt.at[plane, place],
                    edge_send.at[1, i], edge_recv.at[1, i], device,
                ),
                remote(
                    source_in.at[0, :, :, plane, rows], src_edge.at[1 - i],
                    edge_send.at[2, i], edge_recv.at[2, i], device,
                ),
            ]
        return copies

    def plane_tile(i):
        return v.at[0, :, :, edge, pl.ds((PAD + SECTOR, PAD - 8)[i], 8)]

    def tile_copies():
        return [
            remote(
                v.at[1, :, :, edge, pl.ds(at_, 8)], v.at[1, :, :, edge, pl.ds(row, 8)],
                tile_send.at[i], tile_recv.at[i], (y, device, a),
            )
            for i, (at_, row, device) in enumerate(
                ((PAD, PAD + SECTOR, t_prev), (PAD + SECTOR - 8, PAD - 8, t_next))
            )
        ]

    def pack_copy():
        return remote(pack.at[0], pack.at[1], pk_sem.at[0], pk_sem.at[1], (py, t, pa))

    helps = jnp.logical_and(bnd, jnp.logical_not(owner))
    served = jnp.logical_and(owner, paired)

    load_jac.wait()

    def spread(l, carry):
        for d in range(3):
            for w in range(VARS):
                for c in range(VARS):
                    jb[(d * VARS + w) * VARS + c, l] = jnp.broadcast_to(
                        jin[d, w, c, pl.ds(l, 1), :] * 0.5, (8, 128)
                    )
        return carry

    lax.fori_loop(0, LAYERS, spread, 0)
    load_state.wait()
    load_step.wait()

    @pl.when(bnd)
    def _():
        parts[pl.ds(160, 32), :] = dt[edge - 1, PAD : PAD + SECTOR, :]
        forward(0)
        stage_parts(0)

    stage_theta(0)

    pl.semaphore_wait(
        barrier,
        2
        + jnp.where(a > 0, 1, 0)
        + jnp.where(a < nax - 1, 1, 0)
        + jnp.where(
            bnd,
            jnp.where(owner, jnp.where(paired, 2 * nth - 1, nth - 1), nth),
            0,
        ),
    )


    @pl.when(bnd)
    def _():
        copies = edge_copies()
        for copy in copies[::3]:
            copy.start()
        send_parts(0)
        for i in (1, 4, 2, 5):
            copies[i].start()
        pl.when(helps)(lambda: pack_copy().start())

    for copy in theta_copies(0):
        copy.start()
    pl.when(jnp.logical_or(a == 1, a == nax - 1))(lambda: axial_down(0).start())
    pl.when(jnp.logical_or(a == 0, a == nax - 2))(lambda: axial_up(0).start())
    load_source.wait()

    far = (jnp.where(inlet, 3, 2), jnp.where(outlet, LAYERS - 1, LAYERS))
    near = jnp.where(inlet, 1, LAYERS - 1)
    second = jnp.where(inlet, 2, LAYERS - 1)

    for q in (0, 2):

        @pl.when(bnd)
        def _():
            if q == 0:
                for i in range(2):
                    wait_for(plane_tile(i), edge_recv.at[0, i])
            else:
                forward(q)
                stage_parts(q)
                send_parts(q)
            for pair in (middle, sides):
                tile_pair(q, edge, pair)
            forward(q + 1)
            stage_parts(q + 1)
            send_parts(q + 1)
            if q == 0:
                for copy in tile_copies():
                    copy.start()

        if q:
            send_theta(q)
        stencil(q, 2, LAYERS, middle)
        if q == 0:
            pl.when(jnp.logical_and(a > 1, a < nax - 1))(lambda: axial_down(0).start())
            pl.when(jnp.logical_and(a > 0, a < nax - 2))(lambda: axial_up(0).start())
        take_theta(q)
        stencil(q, 2, LAYERS, sides)
        if q == 0:

            @pl.when(served)
            def _():
                pack_copy().wait_recv()
                full_table(1)

        take_axial(q)
        outer_layers(q)
        send_theta(q + 1)
        send_axial(q + 1)
        pl.when(owner)(lambda: serve(q))
        stencil(q + 1, *far, middle)
        if q == 0:

            @pl.when(bnd)
            def _():
                for copy in tile_copies():
                    copy.wait()

        take_theta(q + 1)
        stencil(q + 1, *far, sides)
        take_axial(q + 1)
        outer_layers(q + 1)
        if q == 0:
            send_axial(q + 2)

        @pl.when(bnd)
        def _():
            now = fix_of(q)
            if q == 0:
                for i in range(2):
                    wait_for(dt.at[edge - 1, pl.ds(PAD, 8)], edge_recv.at[1, i])
                    wait_for(src_edge.at[i], edge_recv.at[2, i])
                subtract(q, now, 8)
                for third in range(3):
                    first = PAD - 8 + 16 * third
                    tile_pair(q + 1, edge, (first, first + 8))
                stencil(q + 1, second, second + 1)
                subtract(q + 1, fix_of(q + 1), 8)
            else:
                subtract(q, now, 8)
                stencil(q + 1, near, near + 2)
                subtract(q + 1, fix_of(q + 1), 0)

    for q in range(SECTIONS):
        for copy in theta_copies(q):
            copy.wait_send()
        pl.when(a > 0)(lambda: axial_down(q).wait_send())
        pl.when(a < nax - 1)(lambda: axial_up(q).wait_send())

    @pl.when(bnd)
    def _():
        for copy in edge_copies():
            copy.wait_send()
        pl.when(helps)(lambda: pack_copy().wait_send())
        for q in range(SECTIONS):
            alike = ((sent, p_send, got, c_send), (sent_x, x_send, got_x, y_send))
            for mine, mine_sem, theirs, theirs_sem in alike:
                pl.when(owner)(
                    lambda: wait_for(mine.at[q, pl.ds(0, nth - 1)], mine_sem.at[q])
                )
                pl.when(helps)(lambda: wait_for(mine.at[q], mine_sem.at[q]))
                pl.when(served)(
                    lambda: wait_for(theirs.at[q, pl.ds(0, 2 * nth - 1)], theirs_sem.at[q])
                )
                pl.when(jnp.logical_and(owner, alone))(
                    lambda: wait_for(theirs.at[q, pl.ds(0, nth - 1)], theirs_sem.at[q])
                )
        pl.when(owner)(
            lambda: wait_for(
                sent_x.at[SECTIONS, pl.ds(0, nth - 1)], x_send.at[SECTIONS]
            )
        )
        pl.when(helps)(lambda: wait_for(sent_x.at[SECTIONS], x_send.at[SECTIONS]))


def solution(mesh):
    nrow, nth, nax = mesh.shape["row"], mesh.shape["theta"], mesh.shape["axial"]

    def step(state, source, time_step, jacobian, blade, order, giles, coupling):
        circle = order.shape[1]
        giles = giles.transpose(0, 1, 2, 4, 3, 5)
        coupling = coupling.transpose(0, 1, 3, 2, 4)
        cells = (2, VARS)
        anyspace = pl.BlockSpec(memory_space=pl.ANY)
        scalars = pl.BlockSpec(memory_space=pltpu.SMEM)
        dma = pltpu.SemaphoreType.DMA
        return pl.pallas_call(
            functools.partial(kernel, (nrow, nth, nax, circle)),
            out_shape=pltpu.VMEM(state.shape, F32),
            in_specs=[anyspace] * 7 + [scalars],
            out_specs=pl.BlockSpec(memory_space=pltpu.VMEM),
            scratch_shapes=[
                pltpu.SMEM(order.shape, jnp.int32),
                pltpu.SMEM(giles.shape, F32),
                pltpu.SMEM(coupling.shape, F32),
                pltpu.VMEM((SECTIONS, *cells, LAYERS + 2, 2 * PAD + SECTOR, RADII), F32),
                pltpu.VMEM((*cells, LAYERS, SECTOR, RADII), F32),
                pltpu.VMEM((2, *cells, 8, RADII), F32),
                pltpu.VMEM((LAYERS, 2 * PAD + SECTOR, RADII), F32),
                pltpu.VMEM((3, VARS, VARS, LAYERS, RADII), F32),
                pltpu.VMEM((75, LAYERS, 8, RADII), F32),
                pltpu.VMEM((SECTIONS, 2, *cells, LAYERS, RADII), F32),
                pltpu.VMEM((SECTIONS, 2, *cells, LAYERS, RADII), F32),
                pltpu.VMEM((32, 256), BF16),
                pltpu.VMEM((2 * (SECTOR + 16), 128), BF16),
                pltpu.VMEM((2, 128, 2 * circle), BF16),
                pltpu.VMEM((2, 104, 128), F32),
                pltpu.VMEM((256, 128), F32),
                pltpu.VMEM((SECTIONS, nth, BAND, 128), F32),
                pltpu.VMEM((SECTIONS + 1, nth, 2, 128), F32),
                pltpu.VMEM((SECTIONS, 2 * nth, BAND, 128), F32),
                pltpu.VMEM((SECTIONS, 2 * nth, 2, 128), F32),
                pltpu.VMEM((2 * nth, 2, 128), F32),
                pltpu.VMEM((2, BAND, circle), F32),
                pltpu.VMEM((SECTIONS, 2, BAND, 128), F32),
                pltpu.VMEM((SECTIONS, 2, 2, 128), F32),
                pltpu.VMEM((SECTIONS, nth, BAND, 128), F32),
                pltpu.VMEM((SECTIONS, nth, 2, 128), F32),
                pltpu.VMEM((RADII, 128), F32),
                dma((7,)),
                dma((SECTIONS, 2)),
                dma((SECTIONS, 2)),
                dma((SECTIONS, 2)),
                dma((SECTIONS, 2)),
                dma((3, 2)),
                dma((3, 2)),
                dma((2,)),
                dma((2,)),
                dma((2,)),
                dma((SECTIONS,)),
                dma((SECTIONS, 2)),
                dma((SECTIONS + 1,)),
                dma((SECTIONS + 1, 2)),
                dma((SECTIONS,)),
                dma((SECTIONS,)),
                dma((SECTIONS,)),
                dma((SECTIONS,)),
            ],
            compiler_params=pltpu.CompilerParams(
                collective_id=0, has_side_effects=True, vmem_limit_bytes=VMEM_LIMIT
            ),
        )(
            *(
                pltpu.with_memory_space_constraint(x, pltpu.HBM)
                for x in (state, source, time_step, jacobian, order, giles, coupling)
            ),
            blade,
        )

    return jax.shard_map(
        step,
        mesh=mesh,
        in_specs=(
            P("row", None, None, "axial", "theta", None),
            P("row", None, None, "axial", "theta", None),
            P("row", "axial", "theta", None),
            P("row", None, None, None, "axial", None),
            P("row"),
            P("row", None),
            P("row", None, None, None, None, None),
            P("row", None, None, None, None),
        ),
        out_specs=P("row", None, None, "axial", "theta", None),
        check_vma=False,
    )
```
